32 devices in a mesh: dp: 8 (over y, x, core), rep: 4 (over z).
Axes of the slice: x: 2, y: 2, z: 4, core: 2. Of those that a mesh axis runs over, the one named last changes fastest.
Arguments:
- tokens: bfloat16 [4096, 512], P(('dp', 'rep')), may hold values from -6 to 6
- cotangent: bfloat16 [4096, 512], P(('dp', 'rep')), may hold values from -6 to 6
- seq_lengths: int32 [32, 4], P(('dp', 'rep')), may hold values from 0 to 128, as said below
- query_weight: bfloat16 [512, 512], P('dp'), may hold values from -0.25 to 0.25
- key_weight: bfloat16 [512, 512], P('dp'), may hold values from -0.25 to 0.25
- value_weight: bfloat16 [512, 512], P('dp'), may hold values from -0.25 to 0.25
- output_weight: bfloat16 [512, 512], P('dp'), may hold values from -1 to 1
- inner_weight: bfloat16 [512, 2048], P('dp'), may hold values from -0.25 to 0.25
- outer_weight: bfloat16 [2048, 512], P('dp'), may hold values from -0.125 to 0.125
- query_bias: bfloat16 [512], P('dp'), may hold values from -3 to 3
- value_bias: bfloat16 [512], P('dp'), may hold values from -3 to 3
- output_bias: bfloat16 [512], P('dp'), may hold values from -3 to 3
- inner_bias: bfloat16 [2048], P('dp'), may hold values from -3 to 3
- outer_bias: bfloat16 [512], P('dp'), may hold values from -3 to 3
- first_gain: bfloat16 [512], P('dp'), may hold values from 0.5 to 1.5
- first_shift: bfloat16 [512], P('dp'), may hold values from -3 to 3
- second_gain: bfloat16 [512], P('dp'), may hold values from 0.5 to 1.5
- second_shift: bfloat16 [512], P('dp'), may hold values from -3 to 3
Outputs:
- layer_out: bfloat16 [4096, 512], P(('dp', 'rep'))
- grad_tokens: bfloat16 [4096, 512], P(('dp', 'rep'))
- grad_query_weight: float32 [512, 512], P('dp')
- grad_key_weight: float32 [512, 512], P('dp')
- grad_value_weight: float32 [512, 512], P('dp')
- grad_output_weight: float32 [512, 512], P('dp')
- grad_inner_weight: float32 [512, 2048], P('dp')
- grad_outer_weight: float32 [2048, 512], P('dp')
- grad_query_bias: float32 [512], P('dp')
- grad_value_bias: float32 [512], P('dp')
- grad_output_bias: float32 [512], P('dp')
- grad_inner_bias: float32 [2048], P('dp')
- grad_outer_bias: float32 [512], P('dp')
- grad_first_gain: float32 [512], P('dp')
- grad_first_shift: float32 [512], P('dp')
- grad_second_gain: float32 [512], P('dp')
- grad_second_shift: float32 [512], P('dp')
The draws below stay inside these ranges and needn't reach their ends.
Inputs may be any that keep to these rules, and one draw needn't show every extreme that they name: `seq_lengths`: row b holds the lengths of up to 4 sequences packed one after another from the first row of buffer b, zero for an empty slot; a row sums to at least 64 and at most 128, and rows past the sum are padding. Some buffer holds a single sequence of 128 tokens.
All inputs are finite; a program needn't handle non-finite values.
Results may differ from the reference program's by a relative error of at most 0.02.
Values may be sent and summed in bfloat16 or wider, within the bound.
No kernel may reach another device: no remote copies, remote signals or barrier semaphores. Data moves between devices by JAX's collectives and lax.ppermute only.
A program may use at most 64 MiB of HBM per device.

```python
import math
import jax
import jax.numpy as jnp
from jax import lax

D = 512
FF = 2048
HEADS = 8
HEAD_DIM = 64
TOK_DEV = 128
SLOTS = 4
TOKENS = 4096


def draw_seq_lengths(key, part):
    key = jax.random.fold_in(key, 11)
    first, second, third = jax.random.split(key, 3)
    buffers = TOKENS // TOK_DEV
    used = jax.random.randint(first, (buffers, 1), TOK_DEV // 2, TOK_DEV + 1).astype(jnp.int32)
    cuts = jax.random.randint(second, (buffers, SLOTS - 1), 0, TOK_DEV + 1).astype(jnp.int32)
    cuts = jnp.sort(cuts * used // TOK_DEV, axis=1)
    edges = jnp.concatenate([jnp.zeros((buffers, 1), jnp.int32), cuts, used], axis=1)
    lengths = edges[:, 1:] - edges[:, :-1]
    chosen = jax.random.randint(third, (), 0, buffers)
    single = jnp.concatenate([jnp.full((1,), TOK_DEV, jnp.int32), jnp.zeros((SLOTS - 1,), jnp.int32)])
    picked = (jnp.arange(buffers) == chosen)[:, None]
    return jnp.where(picked, single[None, :], lengths).astype(jnp.int32)


def block_levels(stream_key, extent, shards, least, top_value):
    loudness = 1.0
    for dim, shards_of in shards:
        heights = jax.random.uniform(jax.random.fold_in(jax.random.fold_in(stream_key, 6), dim), (shards_of,), jnp.float32, least / len(shards), top_value / len(shards))
        loudness = loudness * jnp.repeat(jnp.exp(heights), extent[dim] // shards_of).reshape((-1,) + (1,) * (len(extent) - 1 - dim))
    return loudness


def noise(own_key, extent, width, most, cuts=(), kind=jnp.bfloat16):
    values = jax.random.normal(own_key, extent, jnp.float32) * width
    if len(cuts) > 0:
        values = block_levels(own_key, extent, cuts, -0.22, 0.18) * values
    return jnp.clip(values, min=-most, max=most).astype(kind)


def setup_inputs(seed: int = 0) -> dict:
    seeds = jax.random.split(jax.random.key(seed), 19)
    tokens = noise(seeds[0], (TOKENS, D), 1.0, 6.0, ((0, 32),))
    cotangent = noise(seeds[1], (TOKENS, D), 1.0, 6.0, ((0, 32),))
    seq_lengths = draw_seq_lengths(jax.random.fold_in(seeds[18], 71), 0)
    query_weight = noise(seeds[3], (D, D), D ** -0.5, 0.25, ((0, 8),))
    key_weight = noise(seeds[4], (D, D), D ** -0.5, 0.25, ((0, 8),))
    value_weight = noise(seeds[5], (D, D), D ** -0.5, 0.25, ((0, 8),))
    output_weight = noise(seeds[6], (D, D), (D // 16) ** -0.5, 1.0, ((0, 8),))
    inner_weight = noise(seeds[7], (D, FF), D ** -0.5, 0.25, ((0, 8),))
    outer_weight = noise(seeds[8], (FF, D), FF ** -0.5, 0.125, ((0, 8),))
    query_bias = noise(seeds[9], (D,), 0.5, 3.0, ((0, 8),))
    value_bias = noise(seeds[10], (D,), 0.5, 3.0, ((0, 8),))
    output_bias = noise(seeds[11], (D,), 0.5, 3.0, ((0, 8),))
    inner_bias = noise(seeds[12], (FF,), 0.5, 3.0, ((0, 8),))
    outer_bias = noise(seeds[13], (D,), 0.5, 3.0, ((0, 8),))
    first_gain = jnp.clip(1.0 + 0.1 * jax.random.normal(seeds[14], (D,), jnp.float32), 0.5, 1.5).astype(jnp.bfloat16)
    first_shift = noise(seeds[15], (D,), 0.5, 3.0, ((0, 8),))
    second_gain = jnp.clip(1.0 + 0.1 * jax.random.normal(seeds[16], (D,), jnp.float32), 0.5, 1.5).astype(jnp.bfloat16)
    second_shift = noise(seeds[17], (D,), 0.5, 3.0, ((0, 8),))
    return dict(tokens=tokens, cotangent=cotangent, seq_lengths=seq_lengths, query_weight=query_weight, key_weight=key_weight, value_weight=value_weight, output_weight=output_weight, inner_weight=inner_weight, outer_weight=outer_weight, query_bias=query_bias, value_bias=value_bias, output_bias=output_bias, inner_bias=inner_bias, outer_bias=outer_bias, first_gain=first_gain, first_shift=first_shift, second_gain=second_gain, second_shift=second_shift)


EPS = 1e-05
HIGH = lax.Precision.HIGHEST

@jax.custom_vjp
def low(v):
    return lax.optimization_barrier(v.astype(jnp.bfloat16)).astype(jnp.float32)

@jax.custom_vjp
def low_back(v):
    return v

def low_keep(v):
    return (low(v), None)

def low_pass(kept, grad):
    return (grad,)

def back_keep(v):
    return (v, None)

def back_low(kept, grad):
    return (low(grad),)
low.defvjp(low_keep, low_pass)
low_back.defvjp(back_keep, back_low)

def normalize(summed, gain, shift):
    mean = lax.optimization_barrier(jnp.mean(summed, -1, keepdims=True))
    centred = summed - mean
    spread = lax.optimization_barrier(jnp.mean(centred * centred, -1, keepdims=True))
    return centred * lax.rsqrt(spread + EPS) * gain + shift

def project(left, right):
    return jnp.einsum('gtd,de->gte', left, right, precision=HIGH)

def layer(params, inputs, valid, segment):
    query_weight, key_weight, value_weight, output_weight, inner_weight, outer_weight, query_bias, value_bias, output_bias, inner_bias, outer_bias, first_gain, first_shift, second_gain, second_shift = params
    blocks, rows = (inputs.shape[0], inputs.shape[1])
    shaped = (blocks, rows, HEADS, HEAD_DIM)
    rounded = low(inputs)
    queries = low(low_back(project(rounded, query_weight) + query_bias)).reshape(shaped)
    key_rows = low(low_back(project(rounded, key_weight))).reshape(shaped)
    value_rows = low(low_back(project(rounded, value_weight) + value_bias)).reshape(shaped)
    raw = jnp.einsum('gqhd,gkhd->ghqk', queries, key_rows, precision=HIGH)
    scores = low_back(raw * HEAD_DIM ** (-0.5))
    same = segment[:, :, None] == segment[:, None, :]
    scores = jnp.where(same[:, None], scores, -1e+30)
    probs = low(jax.nn.softmax(scores, axis=-1))
    mixed = jnp.einsum('ghqk,gkhd->gqhd', probs, value_rows, precision=HIGH).reshape(inputs.shape)
    attended = low(low_back(mixed))
    branch = low_back(project(attended, output_weight) + output_bias)
    first_out = normalize(inputs + branch, first_gain, first_shift)
    inner = low_back(project(low(first_out), inner_weight) + inner_bias)
    activated = low(jax.nn.gelu(inner, approximate=False))
    outer = low_back(project(activated, outer_weight) + outer_bias)
    return valid[..., None] * normalize(first_out + outer, second_gain, second_shift)

def reference(tokens, cotangent, seq_lengths, query_weight, key_weight, value_weight, output_weight, inner_weight, outer_weight, query_bias, value_bias, output_bias, inner_bias, outer_bias, first_gain, first_shift, second_gain, second_shift):
    params = tuple((piece.astype(jnp.float32) for piece in (query_weight, key_weight, value_weight, output_weight, inner_weight, outer_weight, query_bias, value_bias, output_bias, inner_bias, outer_bias, first_gain, first_shift, second_gain, second_shift)))
    buffers = TOKENS // TOK_DEV
    group = math.gcd(buffers, max(1, 4096 // TOK_DEV))
    rounds = buffers // group
    ends = jnp.cumsum(seq_lengths, axis=1).astype(jnp.int32)
    places = jnp.arange(TOK_DEV, dtype=jnp.int32)
    segment = lax.optimization_barrier(jnp.sum((places[None, :, None] >= ends[:, None, :]).astype(jnp.int32), axis=-1)).astype(jnp.int32)
    valid = (places[None, :] < ends[:, -1:]).astype(jnp.float32)
    inputs = tokens.astype(jnp.float32).reshape(rounds, group, TOK_DEV, D)
    upstream = cotangent.astype(jnp.float32).reshape(rounds, group, TOK_DEV, D)

    def advance(totals, pieces):
        block_in, block_up, block_valid, block_segment = pieces
        result, back = jax.vjp(lambda held, given: layer(held, given, block_valid, block_segment), params, block_in)
        grad_params, grad_in = back(block_up)
        totals = jax.tree.map(jnp.add, totals, grad_params)
        return (totals, (result.astype(jnp.bfloat16), grad_in.astype(jnp.bfloat16)))
    zeros = jax.tree.map(jnp.zeros_like, params)
    totals, (results, grads_in) = lax.scan(advance, zeros, (inputs, upstream, valid.reshape(rounds, group, TOK_DEV), segment.reshape(rounds, group, TOK_DEV)))
    return (results.reshape(TOKENS, D), grads_in.reshape(TOKENS, D), totals[0], totals[1], totals[2], totals[3], totals[4], totals[5], totals[6], totals[7], totals[8], totals[9], totals[10], totals[11], totals[12], totals[13], totals[14])
```

```python
import functools

import jax
import jax.numpy as jnp
from jax import lax
from jax.experimental import pallas as pl
from jax.experimental.pallas import tpu as pltpu
from jax.sharding import PartitionSpec as P

HEADS = 8
HEAD_DIM = 64
EPS = 1e-05
SMALL_ROWS = 16
BF16 = jnp.bfloat16
F32 = jnp.float32
VMEM_LIMIT = 48 * 1024 * 1024


def dot(left, right):
    return lax.dot_general(left, right, (((1,), (0,)), ((), ())), preferred_element_type=F32)


def dot_rt(left, right):
    return lax.dot_general(left, right, (((1,), (1,)), ((), ())), preferred_element_type=F32)


def dot_lt(left, right):
    return lax.dot_general(left, right, (((0,), (0,)), ((), ())), preferred_element_type=F32)


def mean_of(values):
    return jnp.mean(values, -1, keepdims=True)


def normalize(summed):
    centred = summed - mean_of(summed)
    scale = lax.rsqrt(mean_of(centred * centred) + EPS)
    return centred * scale, scale


def norm_back(grad_normed, normed, scale):
    return scale * (grad_normed - mean_of(grad_normed) - normed * mean_of(grad_normed * normed))


def row_sum(values):
    return jnp.sum(values, 0, keepdims=True)


class Shards:
    def __init__(self, pieces, stacked):
        self.pieces = pieces
        self.stacked = stacked

    def operands(self):
        return list(self.pieces)

    def take(self, refs, groups):
        if self.stacked:
            return [refs[0].at[index] for index in range(groups)], False
        return list(refs), True


def load_shards(me, sources, relative, copies, sems, base):
    started = []
    count = base
    for index, source in enumerate(sources):
        owner = (me ^ index) if relative else index
        for first, size, target in copies:
            place = target.at[pl.ds(owner * size if not relative else pl.multiple_of(owner * size, size), size)]
            copy = pltpu.make_async_copy(source.at[pl.ds(first, size)], place, sems.at[count])
            copy.start()
            started.append(copy)
            count += 1
    return started, count


def ends_of(len_ref, slots):
    ends = []
    total = jnp.int32(0)
    for slot in range(slots):
        total = total + len_ref[0, slot]
        ends.append(total)
    return ends


def valid_rows(len_ref, rows):
    ends = ends_of(len_ref, len_ref.shape[1])
    places = lax.broadcasted_iota(jnp.int32, (rows, 1), 0)
    return (places < ends[-1]).astype(F32)


def forward_attention_kernel(
    groups, shards, me_ref, len_ref, tok_ref, *refs
):
    first_sources, relative = shards[0].take(refs[: len(shards[0].pieces)], groups)
    refs = refs[len(shards[0].pieces) :]
    second_sources, _ = shards[1].take(refs[: len(shards[1].pieces)], groups)
    refs = refs[len(shards[1].pieces) :]
    (query_ref, key_ref, value_ref, probs_ref, normed_ref, scale_ref, vec_ref, mine_ref, other_ref,
     wq, wk, wv, wo, smalls, joined, turned, sems) = refs
    me = me_ref[0]
    rows, width = tok_ref.shape
    part = width // groups
    copies, count = load_shards(
        me, first_sources, relative,
        [(0, part, wq), (part, part, wk), (2 * part, SMALL_ROWS, smalls)], sems, 0)
    more, count = load_shards(
        me, second_sources, relative, [(0, part, wv), (part, part, wo)], sems, count)
    tokens = tok_ref[...]
    ends = ends_of(len_ref, len_ref.shape[1])
    across = lax.broadcasted_iota(jnp.int32, (rows, rows), 1)
    down = lax.broadcasted_iota(jnp.int32, (rows, rows), 0)
    segment_across = jnp.zeros((rows, rows), jnp.int32)
    segment_down = jnp.zeros((rows, rows), jnp.int32)
    for end in ends:
        segment_across = segment_across + (across >= end).astype(jnp.int32)
        segment_down = segment_down + (down >= end).astype(jnp.int32)
    same = segment_across == segment_down
    turned[0] = tokens.astype(F32).T.astype(BF16).reshape(groups // 2, 2, part, rows)
    for copy in copies + more:
        copy.wait()
    ff_part = vec_ref.shape[1] // groups
    vec_ref[...] = jnp.zeros_like(vec_ref)
    for owner in range(groups):
        block = smalls[owner * SMALL_ROWS : (owner + 1) * SMALL_ROWS].astype(F32)
        for row in range(9):
            size = ff_part if row == 3 else part
            vec_ref[row : row + 1, owner * size : (owner + 1) * size] = block[row : row + 1, :size]
    query = (dot(tokens, wq[...]) + vec_ref[0:1, :width]).astype(BF16)
    keys = dot(tokens, wk[...]).astype(BF16)
    values = (dot(tokens, wv[...]) + vec_ref[1:2, :width]).astype(BF16)
    query_ref[...] = query
    key_ref[...] = keys
    value_ref[...] = values
    for head in range(HEADS):
        lanes = slice(head * HEAD_DIM, (head + 1) * HEAD_DIM)
        scores = dot_rt(query[:, lanes], keys[:, lanes]) * HEAD_DIM ** (-0.5)
        scores = jnp.where(same, scores, -1e30)
        raised = jnp.exp(scores - jnp.max(scores, -1, keepdims=True))
        probs = raised / jnp.sum(raised, -1, keepdims=True)
        probs_ref[head] = probs
        joined[:, lanes] = dot(probs.astype(BF16), values[:, lanes]).astype(BF16)
    attended = joined[...]
    summed = tokens.astype(F32) + dot(attended, wo[...]) + vec_ref[2:3, :width]
    normed, scale = normalize(summed)
    normed_ref[...] = normed
    scale_ref[...] = scale
    first_low = normed * vec_ref[5:6, :width] + vec_ref[6:7, :width]
    turned[1] = attended.astype(F32).T.astype(BF16).reshape(groups // 2, 2, part, rows)
    turned[2] = first_low.astype(BF16).astype(F32).T.astype(BF16).reshape(groups // 2, 2, part, rows)
    core = me & 1
    for kind in range(3):
        for block in range(groups // 2):
            mine_ref[kind, block] = turned[kind, block, core]
            other_ref[kind, block] = turned[kind, block, 1 - core]


def forward_hidden_kernel(groups, shards, me_ref, len_ref, normed_ref, vec_ref, cot_ref, *refs):
    inner_sources, relative = shards[0].take(refs[: len(shards[0].pieces)], groups)
    refs = refs[len(shards[0].pieces) :]
    outer_sources, _ = shards[1].take(refs[: len(shards[1].pieces)], groups)
    refs = refs[len(shards[1].pieces) :]
    (out_ref, slope_ref, grad_ref, low_ref, mine_ref, other_ref, sums_ref,
     wi, wo, kept, sems) = refs
    me = me_ref[0]
    rows, width = normed_ref.shape
    hidden = vec_ref.shape[1]
    part = width // groups
    ff_part = hidden // groups
    copies, count = load_shards(me, inner_sources, relative, [(0, part, wi)], sems, 0)
    more, count = load_shards(me, outer_sources, relative, [(0, ff_part, wo)], sems, count)
    first_out = normed_ref[...] * vec_ref[5:6, :width] + vec_ref[6:7, :width]
    for copy in copies:
        copy.wait()
    first_low = first_out.astype(BF16)
    core = me & 1
    step = min(512, hidden)
    for start in range(0, hidden, step):
        lanes = slice(start, start + step)
        inner = dot(first_low, wi[:, lanes]) + vec_ref[3:4, lanes]
        below = 0.5 * (1.0 + lax.erf(inner * 0.7071067811865476))
        slope_ref[:, lanes] = below + inner * jnp.exp(-0.5 * inner * inner) * 0.3989422804014327
        activated = (inner * below).astype(BF16)
        for owner in range(start // ff_part, (start + step) // ff_part):
            first = owner * ff_part - start
            kept[owner // 2, owner % 2] = activated[:, first : first + ff_part]
    for copy in more:
        copy.wait()
    second_sum = first_out + vec_ref[4:5, :width]
    for owner in range(groups):
        second_sum = second_sum + dot(
            kept[owner // 2, owner % 2], wo[owner * ff_part : (owner + 1) * ff_part])
    normed, scale = normalize(second_sum)
    valid = valid_rows(len_ref, rows)
    gain = vec_ref[7:8, :width]
    out_ref[...] = (valid * (normed * gain + vec_ref[8:9, :width])).astype(BF16)
    upstream = cot_ref[...].astype(F32) * valid
    grad = norm_back(upstream * gain, normed, scale)
    low = grad.astype(BF16)
    grad_ref[...] = grad
    low_ref[...] = low
    sums_ref[0:1] = row_sum(low.astype(F32))
    sums_ref[1:2] = row_sum(upstream * normed)
    sums_ref[2:3] = row_sum(upstream)
    for block in range(groups // 2):
        mine_ref[block] = kept[block, core]
        other_ref[block] = kept[block, 1 - core]


def backward_hidden_kernel(
    groups, shards, me_ref, low_ref, slope_ref, grad_ref, normed_ref, scale_ref, vec_ref, *refs
):
    inner_sources, relative = shards[0].take(refs[: len(shards[0].pieces)], groups)
    refs = refs[len(shards[0].pieces) :]
    outer_sources, _ = shards[1].take(refs[: len(shards[1].pieces)], groups)
    refs = refs[len(shards[1].pieces) :]
    second_sources, _ = shards[2].take(refs[: len(shards[2].pieces)], groups)
    refs = refs[len(shards[2].pieces) :]
    (hidden_ref, branch_ref, first_ref, att_ref, sums_ref, hidden_sum_ref,
     wi, wo, wb, sems) = refs
    me = me_ref[0]
    rows, width = normed_ref.shape
    hidden = vec_ref.shape[1]
    part = width // groups
    ff_part = hidden // groups
    copies, count = load_shards(me, outer_sources, relative, [(0, ff_part, wo)], sems, 0)
    more, count = load_shards(me, inner_sources, relative, [(0, part, wi)], sems, count)
    last, count = load_shards(me, second_sources, relative, [(part, part, wb)], sems, count)
    low = low_ref[...]
    for copy in copies:
        copy.wait()
    step = min(512, hidden)
    for start in range(0, hidden, step):
        lanes = slice(start, start + step)
        inner_low = (dot_rt(low, wo[lanes]) * slope_ref[:, lanes]).astype(BF16)
        hidden_ref[:, lanes] = inner_low
        hidden_sum_ref[:, lanes] = row_sum(inner_low.astype(F32))
    for copy in more:
        copy.wait()
    normed = normed_ref[...]
    grad_out = grad_ref[...] + dot_rt(hidden_ref[...], wi[...])
    sums_ref[0:1] = row_sum(grad_out * normed)
    sums_ref[1:2] = row_sum(grad_out)
    grad_first = norm_back(grad_out * vec_ref[5:6, :width], normed, scale_ref[...])
    branch = grad_first.astype(BF16)
    sums_ref[2:3] = row_sum(branch.astype(F32))
    first_ref[...] = grad_first
    branch_ref[...] = branch
    for copy in last:
        copy.wait()
    att_ref[...] = dot_rt(branch, wb[...]).astype(BF16)


def backward_attention_kernel(
    groups, me_ref, query_ref, key_ref, value_ref, probs_ref, att_ref,
    second_sums, first_sums, hidden_sums, grads_ref, mine_ref, other_ref, packed
):
    rows, width = query_ref.shape
    hidden = hidden_sums.shape[1]
    part = width // groups
    ff_part = hidden // groups
    for head in range(HEADS):
        lanes = slice(head * HEAD_DIM, (head + 1) * HEAD_DIM)
        grad_att = att_ref[:, lanes]
        probs = probs_ref[head]
        grad_probs = dot_rt(grad_att, value_ref[:, lanes])
        mixed = probs * grad_probs
        grad_scores = (mixed - probs * jnp.sum(mixed, -1, keepdims=True)).astype(BF16)
        scale = HEAD_DIM ** (-0.5)
        for kind, grad in enumerate((
            scale * dot(grad_scores, key_ref[:, lanes]),
            scale * dot_lt(grad_scores, query_ref[:, lanes]),
            dot_lt(probs.astype(BF16), grad_att),
        )):
            first = kind * width + head * HEAD_DIM
            grads_ref[:, first : first + HEAD_DIM] = grad.astype(BF16)
    packed[...] = jnp.zeros_like(packed)
    query_sum = row_sum(grads_ref[:, :width].astype(F32))
    value_sum = row_sum(grads_ref[:, 2 * width :].astype(F32))
    ordered = (
        query_sum, value_sum, first_sums[2:3], hidden_sums[0:1], second_sums[0:1],
        first_sums[0:1], first_sums[1:2], second_sums[1:2], second_sums[2:3])
    for owner in range(groups):
        for row, vector in enumerate(ordered):
            size = ff_part if row == 3 else part
            packed[owner // 2, owner % 2, row : row + 1, :size] = vector[
                :, owner * size : (owner + 1) * size]
    core = me_ref[0] & 1
    for block in range(groups // 2):
        mine_ref[block] = packed[block, core]
        other_ref[block] = packed[block, 1 - core].astype(BF16)


def grad_tokens_kernel(groups, shards, me_ref, grads_ref, first_ref, *refs):
    first_sources, relative = shards[0].take(refs[: len(shards[0].pieces)], groups)
    refs = refs[len(shards[0].pieces) :]
    second_sources, _ = shards[1].take(refs[: len(shards[1].pieces)], groups)
    refs = refs[len(shards[1].pieces) :]
    out_ref, wq, wk, wv, sems = refs
    me = me_ref[0]
    rows, width = first_ref.shape
    part = width // groups
    copies, count = load_shards(
        me, first_sources, relative, [(0, part, wq), (part, part, wk)], sems, 0)
    more, count = load_shards(me, second_sources, relative, [(0, part, wv)], sems, count)
    for copy in copies + more:
        copy.wait()
    total = first_ref[...]
    for kind, weight in enumerate((wq, wk, wv)):
        total = total + dot_rt(grads_ref[:, kind * width : (kind + 1) * width], weight[...])
    out_ref[...] = total.astype(BF16)


def split_blocks(blocks, slot, half, value, refs):
    if blocks != 4:
        refs[0][slot] = value.astype(refs[0].dtype) if half is None else value
        return
    send_x, keep_x, send_y, keep_y = refs
    if half == 0:
        target, place = (send_x if slot & 1 else keep_x), slot >> 1
    else:
        target, place = (send_y if slot & 2 else keep_y), slot & 1
    target[place] = value.astype(target.dtype)


def outer_grad_kernel(blocks, me_ref, mine_ref, given_ref, low_ref, low_given_ref, *refs):
    first = me_ref[0] >> 1 if blocks == 4 else 0
    low = jnp.concatenate([low_ref[...], low_given_ref[...]], 0)
    for slot in range(blocks):
        block = slot ^ first
        acts = jnp.concatenate([mine_ref[block], given_ref[block]], 0)
        grad = dot_lt(acts, low)
        if blocks == 4:
            half = grad.shape[0] // 2
            split_blocks(blocks, slot, 0, grad[:half], refs)
            split_blocks(blocks, slot, 1, grad[half:], refs)
        else:
            refs[0][slot] = grad.astype(BF16)


def inner_grad_kernel(blocks, me_ref, mine_ref, given_ref, low_ref, low_given_ref, *refs):
    first = me_ref[0] >> 1 if blocks == 4 else 0
    left = jnp.concatenate([
        jnp.concatenate([mine_ref[2, slot ^ first], given_ref[2, slot ^ first]], 1)
        for slot in range(blocks)], 0)
    part = left.shape[0] // blocks
    step = 512
    for start in range(0, low_ref.shape[1], step):
        lanes = slice(start, start + step)
        low = jnp.concatenate([low_ref[:, lanes], low_given_ref[:, lanes]], 0)
        grad = dot(left, low)
        for slot in range(blocks):
            rows = grad[slot * part : (slot + 1) * part]
            if blocks == 4:
                half = part // 2
                send_x, keep_x, send_y, keep_y = refs
                for value, target, place in (
                    (rows[:half], send_x if slot & 1 else keep_x, slot >> 1),
                    (rows[half:], send_y if slot & 2 else keep_y, slot & 1),
                ):
                    target[place, :, lanes] = value.astype(target.dtype)
            else:
                refs[0][slot, :, lanes] = rows.astype(BF16)


def attention_grad_kernel(
    blocks, me_ref, mine_ref, given_ref, grads_ref, grads_given_ref, branch_ref, branch_given_ref,
    small_ref, small_given_ref, *refs
):
    first = me_ref[0] >> 1 if blocks == 4 else 0
    width = branch_ref.shape[1]
    lefts = [
        jnp.concatenate([
            jnp.concatenate([mine_ref[kind, slot ^ first], given_ref[kind, slot ^ first]], 1)
            for slot in range(blocks)], 0)
        for kind in range(2)]
    part = lefts[0].shape[0] // blocks
    products = []
    for kind in range(3):
        lanes = slice(kind * width, (kind + 1) * width)
        right = jnp.concatenate([grads_ref[:, lanes], grads_given_ref[:, lanes]], 0)
        products.append(dot(lefts[0], right))
    products.append(dot(lefts[1], jnp.concatenate([branch_ref[...], branch_given_ref[...]], 0)))
    for slot in range(blocks):
        rows = [grad[slot * part : (slot + 1) * part] for grad in products]
        small = small_ref[slot ^ first] + small_given_ref[slot ^ first].astype(F32)
        halves = ((rows[0], rows[1], small), (rows[2], rows[3]))
        for half, pieces in enumerate(halves):
            if blocks == 4:
                send_x, keep_x, send_y, keep_y = refs
                if half == 0:
                    target, place = (send_x if slot & 1 else keep_x), slot >> 1
                else:
                    target, place = (send_y if slot & 2 else keep_y), slot & 1
            else:
                target, place = refs[half], slot
            start = 0
            for piece in pieces:
                size = piece.shape[0]
                target[place, start : start + size] = piece.astype(target.dtype)
                start += size


ANY = pl.BlockSpec(memory_space=pl.ANY)
VMEM = pl.BlockSpec(memory_space=pltpu.VMEM)
SMEM = pl.BlockSpec(memory_space=pltpu.SMEM)


def call(kernel, in_specs, outs, scratch, name):
    return pl.pallas_call(
        kernel,
        out_shape=[jax.ShapeDtypeStruct(shape, dtype) for shape, dtype in outs],
        in_specs=in_specs,
        out_specs=[VMEM] * len(outs),
        scratch_shapes=scratch,
        compiler_params=pltpu.CompilerParams(vmem_limit_bytes=VMEM_LIMIT),
        name=name,
    )


def flip(groups, mask):
    return [(index, index ^ mask) for index in range(groups)]


def swap(value, groups, mask):
    return lax.ppermute(value, "dp", flip(groups, mask))


def gather(value, groups, by_x):
    if groups != 8:
        return Shards([lax.all_gather(value, "dp", axis=0, tiled=False)], True)
    over_x = swap(value, groups, 2)
    over_y = swap(value, groups, 4)
    over_xy = swap(over_y, groups, 2) if by_x else swap(over_x, groups, 4)
    pieces = []
    for piece in (value, over_x, over_y, over_xy):
        pieces.extend([piece, swap(piece, groups, 1)])
    return Shards(pieces, False)


def group_sum(parts, groups):
    send_x, keep_x, send_y, keep_y = parts
    got_x = swap(send_x, groups, 2)
    got_y = swap(send_y, groups, 4)
    sum_x = keep_x + got_x.astype(F32)
    sum_y = keep_y + got_y.astype(F32)
    last_y = swap(sum_x[1].astype(BF16), groups, 4)
    last_x = swap(sum_y[1].astype(BF16), groups, 2)
    return sum_x[0] + last_y.astype(F32), sum_y[0] + last_x.astype(F32)


def group_sum_any(stacked, groups):
    core = lax.axis_index("dp") & 1
    blocks = groups // 2
    full = jnp.zeros((blocks, 2) + stacked.shape[1:], stacked.dtype)
    full = lax.dynamic_update_slice_in_dim(full, stacked[:, None], core, 1)
    full = full.reshape((groups,) + stacked.shape[1:])
    return lax.psum_scatter(full, "dp", scatter_dimension=0, tiled=False).astype(F32)


def copies_sum(value):
    size = lax.axis_size("rep")
    if size != 4:
        return lax.psum(value.astype(BF16), "rep").astype(F32)
    low = value.astype(BF16)
    got = lax.ppermute(low, "rep", [(0, 1), (1, 0), (2, 3), (3, 2)])
    pair = (low.astype(F32) + got.astype(F32)).astype(BF16)
    got = lax.ppermute(pair, "rep", [(1, 2), (2, 1)])
    total = (pair.astype(F32) + got.astype(F32)).astype(BF16)
    got = lax.ppermute(total, "rep", [(1, 0), (2, 3)])
    place = lax.axis_index("rep")
    inside = (place == 1) | (place == 2)
    return jnp.where(inside, total, got).astype(F32)


def local(
    tokens,
    cotangent,
    seq_lengths,
    query_weight,
    key_weight,
    value_weight,
    output_weight,
    inner_weight,
    outer_weight,
    query_bias,
    value_bias,
    output_bias,
    inner_bias,
    outer_bias,
    first_gain,
    first_shift,
    second_gain,
    second_shift,
):
    groups = lax.axis_size("dp")
    blocks = groups // 2
    rows, width = tokens.shape
    part = width // groups
    ff_part = outer_weight.shape[0]
    hidden = ff_part * groups
    me = lax.axis_index("dp").astype(jnp.int32).reshape(1)
    smalls = (
        query_bias,
        value_bias,
        output_bias,
        inner_bias,
        outer_bias,
        first_gain,
        first_shift,
        second_gain,
        second_shift,
    )
    bucket = jnp.stack(
        [jnp.pad(piece, (0, width - piece.shape[0])) for piece in smalls]
        + [jnp.zeros((width,), BF16)] * (SMALL_ROWS - len(smalls)))
    first = gather(jnp.concatenate([query_weight, key_weight, bucket]), groups, True)
    second = gather(jnp.concatenate([value_weight, output_weight]), groups, False)
    inner = gather(inner_weight, groups, True)
    outer = gather(outer_weight, groups, False)
    weight = (width, width)
    turned = (3, blocks, part, rows)
    query, keys, values, probs, normed, scale, vectors, mine, other = call(
        functools.partial(forward_attention_kernel, groups, (first, second)),
        [SMEM, SMEM, VMEM] + [ANY] * (len(first.pieces) + len(second.pieces)),
        [((rows, width), BF16)] * 3
        + [((HEADS, rows, rows), F32), ((rows, width), F32), ((rows, 1), F32),
           ((SMALL_ROWS, hidden), F32), (turned, BF16), (turned, BF16)],
        [pltpu.VMEM(weight, BF16)] * 4
        + [pltpu.VMEM((groups * SMALL_ROWS, width), BF16), pltpu.VMEM((rows, width), BF16),
           pltpu.VMEM((3, blocks, 2, part, rows), BF16), pltpu.SemaphoreType.DMA((5 * groups,))],
        "forward_attention",
    )(me, seq_lengths, tokens, *first.pieces, *second.pieces)
    given = swap(other, groups, 1)
    acts = (blocks, rows, ff_part)
    layer_out, slope, grad_second, outer_low, act_mine, act_other, second_sums = call(
        functools.partial(forward_hidden_kernel, groups, (inner, outer)),
        [SMEM, SMEM, VMEM, VMEM, VMEM] + [ANY] * (len(inner.pieces) + len(outer.pieces)),
        [((rows, width), BF16), ((rows, hidden), F32), ((rows, width), F32), ((rows, width), BF16),
         (acts, BF16), (acts, BF16), ((8, width), F32)],
        [pltpu.VMEM((width, hidden), BF16), pltpu.VMEM((hidden, width), BF16),
         pltpu.VMEM((blocks, 2, rows, ff_part), BF16), pltpu.SemaphoreType.DMA((2 * groups,))],
        "forward_hidden",
    )(me, seq_lengths, normed, vectors, cotangent, *inner.pieces, *outer.pieces)
    act_given = swap(act_other, groups, 1)
    outer_given = swap(outer_low, groups, 1)

    def grad_call(kernel, specs, halves, name):
        if blocks == 4:
            outs = [((2,) + half, kind) for half in halves for kind in (BF16, F32)]
        elif name == "attention_grad":
            outs = [((blocks,) + half, BF16) for half in halves]
        else:
            whole = (sum(half[0] for half in halves),) + halves[0][1:]
            outs = [((blocks,) + whole, BF16)]
        return call(functools.partial(kernel, blocks), specs, outs, [], name)

    outer_parts = grad_call(
        outer_grad_kernel, [SMEM] + [VMEM] * 4, [(ff_part // 2, width)] * 2, "outer_grad",
    )(me, act_mine, act_given, outer_low, outer_given)
    hidden_low, branch, grad_first, grad_att, first_sums, hidden_sums = call(
        functools.partial(backward_hidden_kernel, groups, (inner, outer, second)),
        [SMEM] + [VMEM] * 6 + [ANY] * (len(inner.pieces) + len(outer.pieces) + len(second.pieces)),
        [((rows, hidden), BF16), ((rows, width), BF16), ((rows, width), F32), ((rows, width), BF16),
         ((8, width), F32), ((1, hidden), F32)],
        [pltpu.VMEM((width, hidden), BF16), pltpu.VMEM((hidden, width), BF16),
         pltpu.VMEM(weight, BF16), pltpu.SemaphoreType.DMA((3 * groups,))],
        "backward_hidden",
    )(me, outer_low, slope, grad_second, normed, scale, vectors,
      *inner.pieces, *outer.pieces, *second.pieces)
    hidden_given = swap(hidden_low, groups, 1)
    branch_given = swap(branch, groups, 1)
    inner_parts = grad_call(
        inner_grad_kernel, [SMEM] + [VMEM] * 4, [(part // 2, hidden)] * 2, "inner_grad",
    )(me, mine, given, hidden_low, hidden_given)
    small = (blocks, SMALL_ROWS, width)
    grads, small_mine, small_other = call(
        functools.partial(backward_attention_kernel, groups),
        [SMEM] + [VMEM] * 8,
        [((rows, 3 * width), BF16), (small, F32), (small, BF16)],
        [pltpu.VMEM((blocks, 2, SMALL_ROWS, width), F32)],
        "backward_attention",
    )(me, query, keys, values, probs, grad_att, second_sums, first_sums, hidden_sums)
    grads_given = swap(grads, groups, 1)
    small_given = swap(small_other, groups, 1)
    attention_parts = grad_call(
        attention_grad_kernel, [SMEM] + [VMEM] * 8,
        [(2 * part + SMALL_ROWS, width), (2 * part, width)], "attention_grad",
    )(me, mine, given, grads, grads_given, branch, branch_given, small_mine, small_given)
    (grad_tokens,) = call(
        functools.partial(grad_tokens_kernel, groups, (first, second)),
        [SMEM, VMEM, VMEM] + [ANY] * (len(first.pieces) + len(second.pieces)),
        [((rows, width), BF16)],
        [pltpu.VMEM(weight, BF16)] * 3 + [pltpu.SemaphoreType.DMA((3 * groups,))],
        "grad_tokens",
    )(me, grads, grad_first, *first.pieces, *second.pieces)

    def owned(parts):
        if blocks == 4:
            summed = jnp.concatenate(group_sum(parts, groups))
        else:
            summed = jnp.concatenate([group_sum_any(piece, groups) for piece in parts])
        return copies_sum(summed)

    grad_outer = owned(outer_parts)
    grad_inner = owned(inner_parts)
    grad_attention = owned(attention_parts)
    at = 2 * part + SMALL_ROWS
    small_rows = grad_attention[2 * part : at]
    return (
        layer_out,
        grad_tokens,
        grad_attention[:part],
        grad_attention[part : 2 * part],
        grad_attention[at : at + part],
        grad_attention[at + part :],
        grad_inner,
        grad_outer,
    ) + tuple(small_rows[row, : piece.shape[0]] for row, piece in enumerate(smalls))


def solution(mesh):
    split = P(("dp", "rep"), None)
    rows = P("dp", None)
    vector = P("dp")
    return jax.shard_map(
        local,
        mesh=mesh,
        in_specs=(split,) * 3 + (rows,) * 6 + (vector,) * 9,
        out_specs=(split,) * 2 + (rows,) * 6 + (vector,) * 9,
        check_vma=False,
    )
```

```python
import functools

import jax
import jax.numpy as jnp
from jax import lax
from jax.experimental import pallas as pl
from jax.experimental.pallas import tpu as pltpu
from jax.sharding import PartitionSpec as P

HEADS = 8
HEAD_DIM = 64
EPS = 1e-05
SMALL_ROWS = 16
BF16 = jnp.bfloat16
F32 = jnp.float32
VMEM_LIMIT = 63 * 1024 * 1024


def dot(left, right):
    return lax.dot_general(left, right, (((1,), (0,)), ((), ())), preferred_element_type=F32)


def dot_rt(left, right):
    return lax.dot_general(left, right, (((1,), (1,)), ((), ())), preferred_element_type=F32)


def dot_lt(left, right):
    return lax.dot_general(left, right, (((0,), (0,)), ((), ())), preferred_element_type=F32)


def mean_of(values):
    return jnp.mean(values, -1, keepdims=True)


def normalize(summed):
    centred = summed - mean_of(summed)
    scale = lax.rsqrt(mean_of(centred * centred) + EPS)
    return centred * scale, scale


def norm_back(grad_normed, normed, scale):
    return scale * (grad_normed - mean_of(grad_normed) - normed * mean_of(grad_normed * normed))


def row_sum(values):
    return jnp.sum(values, 0, keepdims=True)


class Shards:
    def __init__(self, pieces, stacked, hops=()):
        self.pieces = pieces
        self.stacked = stacked
        self.hops = hops

    def operands(self):
        return list(self.pieces)

    def take(self, refs, groups):
        if self.stacked:
            return [refs[0].at[index] for index in range(groups)], False
        return list(refs), True


def load_shards(me, sources, relative, copies, sems, base):
    started = []
    count = base
    for index, source in enumerate(sources):
        owner = (me ^ index) if relative else index
        for first, size, target in copies:
            place = target.at[pl.ds(owner * size if not relative else pl.multiple_of(owner * size, size), size)]
            copy = pltpu.make_async_copy(source.at[pl.ds(first, size)], place, sems.at[count])
            copy.start()
            started.append(copy)
            count += 1
    return started, count


def ends_of(len_ref, slots):
    ends = []
    total = jnp.int32(0)
    for slot in range(slots):
        total = total + len_ref[0, slot]
        ends.append(total)
    return ends


def valid_rows(len_ref, rows):
    ends = ends_of(len_ref, len_ref.shape[1])
    places = lax.broadcasted_iota(jnp.int32, (rows, 1), 0)
    return (places < ends[-1]).astype(F32)


def pack_kernel(count, *refs):
    sources = refs[: 4 + count]
    first_ref, second_ref = refs[4 + count : 6 + count]
    small_refs = refs[6 + count : -1]
    sems = refs[-1]
    part, width = sources[0].shape
    targets = [
        first_ref.at[pl.ds(0, part)], first_ref.at[pl.ds(part, part)],
        second_ref.at[pl.ds(0, part)], second_ref.at[pl.ds(part, part)]] + list(small_refs)
    copies = [
        pltpu.make_async_copy(source, target, sems.at[index])
        for index, (source, target) in enumerate(zip(sources, targets))]
    for copy in copies:
        copy.start()
    for copy in copies:
        copy.wait()
    rows = []
    for small in small_refs:
        values = small[...].astype(F32)
        pieces = [values[row : row + 1] for row in range(values.shape[0])]
        filled = values.shape[0] * values.shape[1]
        rows.append(jnp.concatenate(pieces + [jnp.zeros((1, width - filled), F32)], 1))
    rows.append(jnp.zeros((SMALL_ROWS - len(rows), width), F32))
    first_ref[2 * part :] = jnp.concatenate(rows, 0).astype(BF16)


def forward_attention_kernel(
    groups, shards, me_ref, len_ref, tok_ref, *refs
):
    first_sources, relative = shards[0].take(refs[: len(shards[0].pieces)], groups)
    refs = refs[len(shards[0].pieces) :]
    second_sources, _ = shards[1].take(refs[: len(shards[1].pieces)], groups)
    refs = refs[len(shards[1].pieces) :]
    (query_ref, key_ref, value_ref, probs_ref, normed_ref, scale_ref, vec_ref, mine_ref, other_ref,
     wq, wk, wv, wo, smalls, joined, turned, sems) = refs
    me = me_ref[0]
    rows, width = tok_ref.shape
    part = width // groups
    copies, count = load_shards(
        me, first_sources, relative,
        [(0, part, wq), (part, part, wk), (2 * part, SMALL_ROWS, smalls)], sems, 0)
    more, count = load_shards(
        me, second_sources, relative, [(0, part, wv), (part, part, wo)], sems, count)
    tokens = tok_ref[...]
    ends = ends_of(len_ref, len_ref.shape[1])
    across = lax.broadcasted_iota(jnp.int32, (rows, rows), 1)
    down = lax.broadcasted_iota(jnp.int32, (rows, rows), 0)
    segment_across = jnp.zeros((rows, rows), jnp.int32)
    segment_down = jnp.zeros((rows, rows), jnp.int32)
    for end in ends:
        segment_across = segment_across + (across >= end).astype(jnp.int32)
        segment_down = segment_down + (down >= end).astype(jnp.int32)
    same = segment_across == segment_down
    turned[0] = tokens.astype(F32).T.astype(BF16).reshape(groups // 2, 2, part, rows)
    for copy in copies + more:
        copy.wait()
    ff_part = vec_ref.shape[1] // groups
    vec_ref[...] = jnp.zeros_like(vec_ref)
    for owner in range(groups):
        block = smalls[owner * SMALL_ROWS : (owner + 1) * SMALL_ROWS].astype(F32)
        for row in range(9):
            size = ff_part if row == 3 else part
            vec_ref[row : row + 1, owner * size : (owner + 1) * size] = block[row : row + 1, :size]
    query = (dot(tokens, wq[...]) + vec_ref[0:1, :width]).astype(BF16)
    keys = dot(tokens, wk[...]).astype(BF16)
    values = (dot(tokens, wv[...]) + vec_ref[1:2, :width]).astype(BF16)
    query_ref[...] = query
    key_ref[...] = keys
    value_ref[...] = values
    for head in range(HEADS):
        lanes = slice(head * HEAD_DIM, (head + 1) * HEAD_DIM)
        scores = dot_rt(query[:, lanes], keys[:, lanes]) * HEAD_DIM ** (-0.5)
        scores = jnp.where(same, scores, -1e30)
        raised = jnp.exp(scores - jnp.max(scores, -1, keepdims=True))
        probs = raised * (1.0 / jnp.sum(raised, -1, keepdims=True))
        probs_ref[head] = probs
        joined[:, lanes] = dot(probs.astype(BF16), values[:, lanes]).astype(BF16)
    attended = joined[...]
    summed = tokens.astype(F32) + dot(attended, wo[...]) + vec_ref[2:3, :width]
    normed, scale = normalize(summed)
    normed_ref[...] = normed
    scale_ref[...] = scale
    first_low = normed * vec_ref[5:6, :width] + vec_ref[6:7, :width]
    turned[1] = attended.astype(F32).T.astype(BF16).reshape(groups // 2, 2, part, rows)
    turned[2] = first_low.astype(BF16).astype(F32).T.astype(BF16).reshape(groups // 2, 2, part, rows)
    core = me & 1
    for kind in range(3):
        for block in range(groups // 2):
            mine_ref[kind, block] = turned[kind, block, core]
            other_ref[kind, block] = turned[kind, block, 1 - core]


def forward_hidden_kernel(groups, shards, me_ref, len_ref, normed_ref, vec_ref, cot_ref, *refs):
    inner_sources, relative = shards[0].take(refs[: len(shards[0].pieces)], groups)
    refs = refs[len(shards[0].pieces) :]
    outer_sources, _ = shards[1].take(refs[: len(shards[1].pieces)], groups)
    refs = refs[len(shards[1].pieces) :]
    (out_ref, slope_ref, grad_ref, low_ref, mine_ref, other_ref, sums_ref,
     wi, wo, kept, sems) = refs
    me = me_ref[0]
    rows, width = normed_ref.shape
    hidden = vec_ref.shape[1]
    part = width // groups
    ff_part = hidden // groups
    copies, count = load_shards(me, inner_sources, relative, [(0, part, wi)], sems, 0)
    more, count = load_shards(me, outer_sources, relative, [(0, ff_part, wo)], sems, count)
    first_out = normed_ref[...] * vec_ref[5:6, :width] + vec_ref[6:7, :width]
    for copy in copies:
        copy.wait()
    first_low = first_out.astype(BF16)
    core = me & 1
    step = min(512, hidden)
    for start in range(0, hidden, step):
        lanes = slice(start, start + step)
        inner = dot(first_low, wi[:, lanes]) + vec_ref[3:4, lanes]
        below = 0.5 * (1.0 + lax.erf(inner * 0.7071067811865476))
        slope_ref[:, lanes] = below + inner * jnp.exp(-0.5 * inner * inner) * 0.3989422804014327
        activated = (inner * below).astype(BF16)
        for owner in range(start // ff_part, (start + step) // ff_part):
            first = owner * ff_part - start
            kept[owner // 2, owner % 2] = activated[:, first : first + ff_part]
    for copy in more:
        copy.wait()
    second_sum = first_out + vec_ref[4:5, :width]
    for owner in range(groups):
        second_sum = second_sum + dot(
            kept[owner // 2, owner % 2], wo[owner * ff_part : (owner + 1) * ff_part])
    normed, scale = normalize(second_sum)
    valid = valid_rows(len_ref, rows)
    gain = vec_ref[7:8, :width]
    out_ref[...] = (valid * (normed * gain + vec_ref[8:9, :width])).astype(BF16)
    upstream = cot_ref[...].astype(F32) * valid
    grad = norm_back(upstream * gain, normed, scale)
    low = grad.astype(BF16)
    grad_ref[...] = grad
    low_ref[...] = low
    sums_ref[0:1] = row_sum(low.astype(F32))
    sums_ref[1:2] = row_sum(upstream * normed)
    sums_ref[2:3] = row_sum(upstream)
    for block in range(groups // 2):
        mine_ref[block] = kept[block, core]
        other_ref[block] = kept[block, 1 - core]


def backward_hidden_kernel(
    groups, shards, me_ref, low_ref, slope_ref, grad_ref, normed_ref, scale_ref, vec_ref, *refs
):
    inner_sources, relative = shards[0].take(refs[: len(shards[0].pieces)], groups)
    refs = refs[len(shards[0].pieces) :]
    outer_sources, _ = shards[1].take(refs[: len(shards[1].pieces)], groups)
    refs = refs[len(shards[1].pieces) :]
    second_sources, _ = shards[2].take(refs[: len(shards[2].pieces)], groups)
    refs = refs[len(shards[2].pieces) :]
    (hidden_ref, branch_ref, first_ref, att_ref, sums_ref, hidden_sum_ref,
     wi, wo, wb, sems) = refs
    me = me_ref[0]
    rows, width = normed_ref.shape
    hidden = vec_ref.shape[1]
    part = width // groups
    ff_part = hidden // groups
    copies, count = load_shards(me, outer_sources, relative, [(0, ff_part, wo)], sems, 0)
    more, count = load_shards(me, inner_sources, relative, [(0, part, wi)], sems, count)
    last, count = load_shards(me, second_sources, relative, [(part, part, wb)], sems, count)
    low = low_ref[...]
    for copy in copies:
        copy.wait()
    step = min(512, hidden)
    for start in range(0, hidden, step):
        lanes = slice(start, start + step)
        inner_low = (dot_rt(low, wo[lanes]) * slope_ref[:, lanes]).astype(BF16)
        hidden_ref[:, lanes] = inner_low
        hidden_sum_ref[:, lanes] = row_sum(inner_low.astype(F32))
    for copy in more:
        copy.wait()
    normed = normed_ref[...]
    grad_out = grad_ref[...] + dot_rt(hidden_ref[...], wi[...])
    sums_ref[0:1] = row_sum(grad_out * normed)
    sums_ref[1:2] = row_sum(grad_out)
    grad_first = norm_back(grad_out * vec_ref[5:6, :width], normed, scale_ref[...])
    branch = grad_first.astype(BF16)
    sums_ref[2:3] = row_sum(branch.astype(F32))
    first_ref[...] = grad_first
    branch_ref[...] = branch
    for copy in last:
        copy.wait()
    att_ref[...] = dot_rt(branch, wb[...]).astype(BF16)


def backward_attention_kernel(
    groups, me_ref, query_ref, key_ref, value_ref, probs_ref, att_ref,
    second_sums, first_sums, hidden_sums, grads_ref, mine_ref, other_ref, packed
):
    rows, width = query_ref.shape
    hidden = hidden_sums.shape[1]
    part = width // groups
    ff_part = hidden // groups
    for head in range(HEADS):
        lanes = slice(head * HEAD_DIM, (head + 1) * HEAD_DIM)
        grad_att = att_ref[:, lanes]
        probs = probs_ref[head]
        grad_probs = dot_rt(grad_att, value_ref[:, lanes])
        mixed = probs * grad_probs
        grad_scores = (mixed - probs * jnp.sum(mixed, -1, keepdims=True)).astype(BF16)
        scale = HEAD_DIM ** (-0.5)
        for kind, grad in enumerate((
            scale * dot(grad_scores, key_ref[:, lanes]),
            scale * dot_lt(grad_scores, query_ref[:, lanes]),
            dot_lt(probs.astype(BF16), grad_att),
        )):
            first = kind * width + head * HEAD_DIM
            grads_ref[:, first : first + HEAD_DIM] = grad.astype(BF16)
    packed[...] = jnp.zeros_like(packed)
    query_sum = row_sum(grads_ref[:, :width].astype(F32))
    value_sum = row_sum(grads_ref[:, 2 * width :].astype(F32))
    ordered = (
        query_sum, value_sum, first_sums[2:3], hidden_sums[0:1], second_sums[0:1],
        first_sums[0:1], first_sums[1:2], second_sums[1:2], second_sums[2:3])
    for owner in range(groups):
        for row, vector in enumerate(ordered):
            size = ff_part if row == 3 else part
            packed[owner // 2, owner % 2, row : row + 1, :size] = vector[
                :, owner * size : (owner + 1) * size]
    core = me_ref[0] & 1
    for block in range(groups // 2):
        mine_ref[block] = packed[block, core]
        other_ref[block] = packed[block, 1 - core].astype(BF16)


def grad_tokens_kernel(groups, shards, me_ref, grads_ref, first_ref, *refs):
    first_sources, relative = shards[0].take(refs[: len(shards[0].pieces)], groups)
    refs = refs[len(shards[0].pieces) :]
    second_sources, _ = shards[1].take(refs[: len(shards[1].pieces)], groups)
    refs = refs[len(shards[1].pieces) :]
    out_ref, wq, wk, wv, sems = refs
    me = me_ref[0]
    rows, width = first_ref.shape
    part = width // groups
    copies, count = load_shards(
        me, first_sources, relative, [(0, part, wq), (part, part, wk)], sems, 0)
    more, count = load_shards(me, second_sources, relative, [(0, part, wv)], sems, count)
    for copy in copies + more:
        copy.wait()
    total = first_ref[...]
    for kind, weight in enumerate((wq, wk, wv)):
        total = total + dot_rt(grads_ref[:, kind * width : (kind + 1) * width], weight[...])
    out_ref[...] = total.astype(BF16)


def put(refs, blocks, slot, start, lanes, value):
    ref = refs[slot] if blocks == 4 else refs[0].at[slot]
    ref[start : start + value.shape[0], lanes] = value.astype(ref.dtype)


def outer_grad_kernel(blocks, me_ref, mine_ref, given_ref, low_ref, low_given_ref, *refs):
    first = me_ref[0] >> 1 if blocks == 4 else 0
    low = jnp.concatenate([low_ref[...], low_given_ref[...]], 0)
    for slot in range(blocks):
        block = slot ^ first
        acts = jnp.concatenate([mine_ref[block], given_ref[block]], 0)
        put(refs, blocks, slot, 0, slice(None), dot_lt(acts, low))


def inner_grad_kernel(blocks, me_ref, mine_ref, given_ref, low_ref, low_given_ref, *refs):
    first = me_ref[0] >> 1 if blocks == 4 else 0
    left = jnp.concatenate([
        jnp.concatenate([mine_ref[2, slot ^ first], given_ref[2, slot ^ first]], 1)
        for slot in range(blocks)], 0)
    part = left.shape[0] // blocks
    step = 512
    for start in range(0, low_ref.shape[1], step):
        lanes = slice(start, start + step)
        low = jnp.concatenate([low_ref[:, lanes], low_given_ref[:, lanes]], 0)
        grad = dot(left, low)
        for slot in range(blocks):
            put(refs, blocks, slot, 0, lanes, grad[slot * part : (slot + 1) * part])


def attention_grad_kernel(
    blocks, me_ref, mine_ref, given_ref, grads_ref, grads_given_ref, branch_ref, branch_given_ref,
    small_ref, small_given_ref, *refs
):
    first = me_ref[0] >> 1 if blocks == 4 else 0
    width = branch_ref.shape[1]
    lefts = [
        jnp.concatenate([
            jnp.concatenate([mine_ref[kind, slot ^ first], given_ref[kind, slot ^ first]], 1)
            for slot in range(blocks)], 0)
        for kind in range(2)]
    part = lefts[0].shape[0] // blocks
    for kind in range(4):
        if kind < 3:
            lanes = slice(kind * width, (kind + 1) * width)
            right = jnp.concatenate([grads_ref[:, lanes], grads_given_ref[:, lanes]], 0)
            grad = dot(lefts[0], right)
        else:
            grad = dot(lefts[1], jnp.concatenate([branch_ref[...], branch_given_ref[...]], 0))
        for slot in range(blocks):
            put(refs, blocks, slot, kind * part, slice(None), grad[slot * part : (slot + 1) * part])
    for slot in range(blocks):
        small = small_ref[slot ^ first] + small_given_ref[slot ^ first].astype(F32)
        put(refs, blocks, slot, 4 * part, slice(None), small)


ANY = pl.BlockSpec(memory_space=pl.ANY)
HBM = pl.BlockSpec(memory_space=pltpu.HBM)
VMEM = pl.BlockSpec(memory_space=pltpu.VMEM)
SMEM = pl.BlockSpec(memory_space=pltpu.SMEM)


def call(kernel, in_specs, outs, scratch, name):
    return pl.pallas_call(
        kernel,
        out_shape=[jax.ShapeDtypeStruct(shape, dtype) for shape, dtype in outs],
        in_specs=in_specs,
        out_specs=[VMEM] * len(outs),
        scratch_shapes=scratch,
        compiler_params=pltpu.CompilerParams(vmem_limit_bytes=VMEM_LIMIT),
        cost_estimate=pl.CostEstimate(flops=1, bytes_accessed=1, transcendentals=0),
        name=name,
    )


def after(value, *others):
    return lax.optimization_barrier((value,) + others)[0]


def flip(groups, mask):
    return [(index, index ^ mask) for index in range(groups)]


def swap(value, groups, mask):
    return lax.ppermute(value, "dp", flip(groups, mask))


def first_hops(value, groups):
    if groups != 8:
        return ()
    return swap(value, groups, 2), swap(value, groups, 4)


def gather(value, hops, groups, by_x, *others):
    if groups != 8:
        return Shards([lax.all_gather(value, "dp", axis=0, tiled=False)], True)
    over_x, over_y = hops
    if by_x:
        over_xy = swap(after(over_y, *others), groups, 2)
    else:
        over_xy = swap(after(over_x, *others), groups, 4)
    pieces = []
    for piece in (value, over_x, over_y, over_xy):
        pieces.extend([piece, swap(piece, groups, 1)])
    return Shards(pieces, False)


def group_sum(parts, groups, *others):
    keep = parts[0]
    got = [swap(sent, groups, mask) for mask, sent in zip((2, 4, 6), parts[1:])]
    got = lax.optimization_barrier(tuple(got) + others)[:3]
    return keep + got[0].astype(F32) + got[1].astype(F32) + got[2].astype(F32)


def group_sum_any(stacked, groups):
    core = lax.axis_index("dp") & 1
    blocks = groups // 2
    full = jnp.zeros((blocks, 2) + stacked.shape[1:], stacked.dtype)
    full = lax.dynamic_update_slice_in_dim(full, stacked[:, None], core, 1)
    full = full.reshape((groups,) + stacked.shape[1:])
    return lax.psum_scatter(full, "dp", scatter_dimension=0, tiled=False).astype(F32)


def copies_sum(value):
    place = lax.axis_index("rep")
    size = value.shape[-1] // 4
    value = value.astype(BF16)

    def send(piece, mask):
        return lax.ppermute(piece, "rep", [(index, index ^ mask) for index in range(4)])

    quarters = [
        lax.dynamic_slice_in_dim(value, (place ^ mask) * size, size, value.ndim - 1)
        for mask in range(4)]
    total = quarters[0].astype(F32)
    for mask in (2, 3, 1):
        total = total + send(quarters[mask], mask).astype(F32)
    total = total.astype(BF16)
    one, two, three = [send(total, mask) for mask in (1, 2, 3)]
    odd = (place & 1) == 1
    high = (place & 2) == 2
    lower = (jnp.where(odd, one, total), jnp.where(odd, total, one))
    upper = (jnp.where(odd, three, two), jnp.where(odd, two, three))
    pieces = [jnp.where(high, second, first) for first, second in zip(lower, upper)]
    pieces += [jnp.where(high, first, second) for first, second in zip(lower, upper)]
    return jnp.concatenate(pieces, -1).astype(F32)


class CopiesSum:
    near = [(0, 1), (1, 0), (2, 3), (3, 2)]
    far = [(0, 2), (2, 0), (1, 3), (3, 1)]

    def __init__(self, value):
        self.value = value.astype(BF16)
        self.upper = lax.axis_index("rep") & 1
        self.half = value.shape[0] // 2

    def start(self, *others):
        value = after(self.value, *others)
        self.kept = lax.dynamic_slice_in_dim(value, self.upper * self.half, self.half)
        sent = lax.dynamic_slice_in_dim(value, (1 - self.upper) * self.half, self.half)
        self.got = lax.ppermute(sent, "rep", self.near)

    def cross(self, *others):
        got = after(self.got, *others)
        self.pair = (self.kept.astype(F32) + got.astype(F32)).astype(BF16)
        self.got = lax.ppermute(self.pair, "rep", self.far)
        return self.pair

    def back(self, *others):
        got = after(self.got, *others)
        self.total = (self.pair.astype(F32) + got.astype(F32)).astype(BF16)
        self.got = lax.ppermute(self.total, "rep", self.near)
        return self.total

    def result(self):
        first = jnp.where(self.upper == 0, self.total, self.got)
        second = jnp.where(self.upper == 0, self.got, self.total)
        return jnp.concatenate([first, second]).astype(F32)


def local(
    tokens,
    cotangent,
    seq_lengths,
    query_weight,
    key_weight,
    value_weight,
    output_weight,
    inner_weight,
    outer_weight,
    query_bias,
    value_bias,
    output_bias,
    inner_bias,
    outer_bias,
    first_gain,
    first_shift,
    second_gain,
    second_shift,
):
    groups = lax.axis_size("dp")
    blocks = groups // 2
    rows, width = tokens.shape
    part = width // groups
    ff_part = outer_weight.shape[0]
    hidden = ff_part * groups
    me = lax.axis_index("dp").astype(jnp.int32).reshape(1)
    smalls = (
        query_bias,
        value_bias,
        output_bias,
        inner_bias,
        outer_bias,
        first_gain,
        first_shift,
        second_gain,
        second_shift,
    )
    small_inputs = [
        piece.reshape(max(1, piece.shape[0] // 128), min(128, piece.shape[0])) for piece in smalls]
    first_own, second_own = call(
        functools.partial(pack_kernel, len(smalls)),
        [HBM] * (4 + len(smalls)),
        [((2 * part + SMALL_ROWS, width), BF16), ((2 * part, width), BF16)],
        [pltpu.VMEM(piece.shape, BF16) for piece in small_inputs]
        + [pltpu.SemaphoreType.DMA((4 + len(smalls),))],
        "pack",
    )(query_weight, key_weight, value_weight, output_weight, *small_inputs)
    first_hop = first_hops(first_own, groups)
    second_hop = first_hops(second_own, groups)
    first = gather(first_own, first_hop, groups, True)
    second = gather(second_own, second_hop, groups, False)
    inner_own, outer_own = lax.optimization_barrier(
        (inner_weight, outer_weight, first_own, second_own))[:2]
    inner_hop = first_hops(inner_own, groups)
    outer_hop = first_hops(outer_own, groups)
    inner = gather(inner_own, inner_hop, groups, True)
    outer = gather(outer_own, outer_hop, groups, False)
    weight = (width, width)
    turned = (3, blocks, part, rows)
    query, keys, values, probs, normed, scale, vectors, mine, other = call(
        functools.partial(forward_attention_kernel, groups, (first, second)),
        [SMEM, SMEM, VMEM] + [ANY] * (len(first.pieces) + len(second.pieces)),
        [((rows, width), BF16)] * 3
        + [((HEADS, rows, rows), F32), ((rows, width), F32), ((rows, 1), F32),
           ((SMALL_ROWS, hidden), F32), (turned, BF16), (turned, BF16)],
        [pltpu.VMEM(weight, BF16)] * 4
        + [pltpu.VMEM((groups * SMALL_ROWS, width), BF16), pltpu.VMEM((rows, width), BF16),
           pltpu.VMEM((3, blocks, 2, part, rows), BF16), pltpu.SemaphoreType.DMA((5 * groups,))],
        "forward_attention",
    )(me, seq_lengths, after(tokens, *inner_hop, *outer_hop), *first.pieces, *second.pieces)
    given = swap(other, groups, 1)
    acts = (blocks, rows, ff_part)
    layer_out, slope, grad_second, outer_low, act_mine, act_other, second_sums = call(
        functools.partial(forward_hidden_kernel, groups, (inner, outer)),
        [SMEM, SMEM, VMEM, VMEM, VMEM] + [ANY] * (len(inner.pieces) + len(outer.pieces)),
        [((rows, width), BF16), ((rows, hidden), F32), ((rows, width), F32), ((rows, width), BF16),
         (acts, BF16), (acts, BF16), ((8, width), F32)],
        [pltpu.VMEM((width, hidden), BF16), pltpu.VMEM((hidden, width), BF16),
         pltpu.VMEM((blocks, 2, rows, ff_part), BF16), pltpu.SemaphoreType.DMA((2 * groups,))],
        "forward_hidden",
    )(me, seq_lengths, normed, vectors, cotangent, *inner.pieces, *outer.pieces)
    act_given = swap(act_other, groups, 1)
    outer_given = swap(outer_low, groups, 1)

    def grad_call(kernel, specs, shape, name):
        if blocks == 4:
            outs = [(shape, F32)] + [(shape, BF16)] * 3
        else:
            outs = [((blocks,) + shape, BF16)]
        return call(functools.partial(kernel, blocks), specs, outs, [], name)

    outer_parts = grad_call(
        outer_grad_kernel, [SMEM] + [VMEM] * 4, (ff_part, width), "outer_grad",
    )(me, act_mine, act_given, outer_low, outer_given)
    hidden_low, branch, grad_first, grad_att, first_sums, hidden_sums = call(
        functools.partial(backward_hidden_kernel, groups, (inner, outer, second)),
        [SMEM] + [VMEM] * 6 + [ANY] * (len(inner.pieces) + len(outer.pieces) + len(second.pieces)),
        [((rows, hidden), BF16), ((rows, width), BF16), ((rows, width), F32), ((rows, width), BF16),
         ((8, width), F32), ((1, hidden), F32)],
        [pltpu.VMEM((width, hidden), BF16), pltpu.VMEM((hidden, width), BF16),
         pltpu.VMEM(weight, BF16), pltpu.SemaphoreType.DMA((3 * groups,))],
        "backward_hidden",
    )(me, after(outer_low, outer_parts[0]), slope, grad_second, normed, scale, vectors,
      *inner.pieces, *outer.pieces, *second.pieces)
    hidden_given = swap(hidden_low, groups, 1)
    branch_given = swap(branch, groups, 1)
    small = (blocks, SMALL_ROWS, width)
    grads, small_mine, small_other = call(
        functools.partial(backward_attention_kernel, groups),
        [SMEM] + [VMEM] * 8,
        [((rows, 3 * width), BF16), (small, F32), (small, BF16)],
        [pltpu.VMEM((blocks, 2, SMALL_ROWS, width), F32)],
        "backward_attention",
    )(me, query, keys, values, probs, grad_att, second_sums, first_sums, hidden_sums)
    grads_given = swap(grads, groups, 1)
    small_given = swap(small_other, groups, 1)
    direct = groups == 8 and lax.axis_size("rep") == 4
    waited = ()
    if direct:
        first_sum = group_sum(outer_parts, groups, grads)
        first_copies = CopiesSum(first_sum)
        waited = (first_sum,)
    inner_parts = grad_call(
        inner_grad_kernel, [SMEM] + [VMEM] * 4, (part, hidden), "inner_grad",
    )(me, mine, given, after(hidden_low, *waited), hidden_given)
    if direct:
        first_copies.start(inner_parts[0])
    attention_parts = grad_call(
        attention_grad_kernel, [SMEM] + [VMEM] * 8,
        (4 * part + SMALL_ROWS, width), "attention_grad",
    )(me, mine, given, grads, grads_given, branch, branch_given, small_mine, small_given)
    if direct:
        first_pair = first_copies.cross(attention_parts[0])
        second_sum = group_sum(inner_parts, groups, first_pair)
        second_copies = CopiesSum(second_sum)
        second_copies.start()
        waited = (second_copies.kept,)
    (grad_tokens,) = call(
        functools.partial(grad_tokens_kernel, groups, (first, second)),
        [SMEM, VMEM, VMEM] + [ANY] * (len(first.pieces) + len(second.pieces)),
        [((rows, width), BF16)],
        [pltpu.VMEM(weight, BF16)] * 3 + [pltpu.SemaphoreType.DMA((3 * groups,))],
        "grad_tokens",
    )(me, after(grads, *waited), grad_first, *first.pieces, *second.pieces)

    if direct:
        first_total = first_copies.back(grad_tokens)
        second_pair = second_copies.cross(first_total)
        third_sum = group_sum(attention_parts, groups, second_pair)
        grad_attention = copies_sum(third_sum)
        second_copies.back(third_sum)
        grad_outer, grad_inner = first_copies.result(), second_copies.result()
    else:
        grad_outer, grad_inner, grad_attention = [
            lax.psum(group_sum_any(piece[0], groups).astype(BF16), "rep").astype(F32)
            for piece in (outer_parts, inner_parts, attention_parts)]
    return (
        layer_out,
        grad_tokens,
        grad_attention[:part],
        grad_attention[part : 2 * part],
        grad_attention[2 * part : 3 * part],
        grad_attention[3 * part : 4 * part],
        grad_inner,
        grad_outer,
    ) + tuple(grad_attention[4 * part + row, : piece.shape[0]] for row, piece in enumerate(smalls))


def solution(mesh):
    split = P(("dp", "rep"), None)
    rows = P("dp", None)
    vector = P("dp")
    return jax.shard_map(
        local,
        mesh=mesh,
        in_specs=(split,) * 3 + (rows,) * 6 + (vector,) * 9,
        out_specs=(split,) * 2 + (rows,) * 6 + (vector,) * 9,
        check_vma=False,
    )
```

```python
import functools

import jax
import jax.numpy as jnp
from jax import lax
from jax.experimental import pallas as pl
from jax.experimental.pallas import tpu as pltpu
from jax.sharding import PartitionSpec as P

HEADS = 8
HEAD_DIM = 64
EPS = 1e-05
SMALL_ROWS = 16
BF16 = jnp.bfloat16
F32 = jnp.float32
VMEM_LIMIT = 56 * 1024 * 1024


def dot(left, right):
    return lax.dot_general(left, right, (((1,), (0,)), ((), ())), preferred_element_type=F32)


def dot_rt(left, right):
    return lax.dot_general(left, right, (((1,), (1,)), ((), ())), preferred_element_type=F32)


def dot_lt(left, right):
    return lax.dot_general(left, right, (((0,), (0,)), ((), ())), preferred_element_type=F32)


def mean_of(values):
    return jnp.mean(values, -1, keepdims=True)


def normalize(summed):
    centred = summed - mean_of(summed)
    scale = lax.rsqrt(mean_of(centred * centred) + EPS)
    return centred * scale, scale


def norm_back(grad_normed, normed, scale):
    return scale * (grad_normed - mean_of(grad_normed) - normed * mean_of(grad_normed * normed))


def row_sum(values):
    return jnp.sum(values, 0, keepdims=True)


class Shards:
    def __init__(self, arrays, places, stacked):
        self.arrays = arrays
        self.places = places
        self.stacked = stacked

    def used(self, kinds):
        if self.stacked:
            return [0]
        return sorted({index for kind in kinds for index, _ in self.places[kind]})

    def operands(self, *kinds):
        return [self.arrays[index] for index in self.used(kinds)]

    def sources(self, refs, groups, *kinds):
        used = self.used(kinds)
        if self.stacked:
            return [[(refs[0].at[index], self.places[kind]) for index in range(groups)]
                    for kind in kinds], refs[1:]
        found = dict(zip(used, refs))
        return [[(found[index], row) for index, row in self.places[kind]]
                for kind in kinds], refs[len(used) :]


def load(me, sources, relative, pieces, sems, base):
    copies = []
    for index, (source, start) in enumerate(sources):
        owner = (me ^ index) if relative else index
        for first, size, target, column in pieces:
            place = owner * size
            if relative:
                place = pl.multiple_of(place, size)
            where = target.at[pl.ds(place, size)]
            if column is not None:
                where = target.at[pl.ds(place, size), pl.ds(*column)]
            copies.append(pltpu.make_async_copy(
                source.at[pl.ds(start + first, size)], where, sems.at[base + len(copies)]))
    return copies


def inner_pieces(part, wi):
    width = wi.shape[0]
    return [(index * part, part, wi, (index * width, width))
            for index in range(wi.shape[1] // width)]


def ends_of(len_ref, slots):
    ends = []
    total = jnp.int32(0)
    for slot in range(slots):
        total = total + len_ref[0, slot]
        ends.append(total)
    return ends


def valid_rows(len_ref, rows):
    ends = ends_of(len_ref, len_ref.shape[1])
    places = lax.broadcasted_iota(jnp.int32, (rows, 1), 0)
    return (places < ends[-1]).astype(F32)


def pack_kernel(count, *refs):
    sources = refs[: 4 + count]
    inner_ref, outer_ref = refs[4 + count : 6 + count]
    outs = refs[6 + count : 10 + count]
    small_refs = refs[10 + count : -1]
    sems = refs[-1]
    part, width = sources[0].shape
    first_ref, with_inner_ref, with_outer_ref, blocked_ref = outs
    start = first_ref.shape[0]
    pairs = []
    for index in range(inner_ref.shape[1] // width):
        for target, row in ((blocked_ref, 0), (with_inner_ref, start)):
            pairs.append((
                inner_ref.at[:, pl.ds(index * width, width)],
                target.at[pl.ds(row + index * part, part)]))
    for index, source in enumerate(sources[:4]):
        for target in outs[:3]:
            pairs.append((source, target.at[pl.ds(index * part, part)]))
    pairs += list(zip(sources[4:], small_refs))
    pairs.append((outer_ref, with_outer_ref.at[pl.ds(start, outer_ref.shape[0])]))
    copies = [
        pltpu.make_async_copy(source, target, sems.at[index])
        for index, (source, target) in enumerate(pairs)]
    for copy in copies:
        copy.start()
    for copy in copies:
        copy.wait()
    rows = []
    for small in small_refs:
        values = small[...].astype(F32)
        pieces = [values[row : row + 1] for row in range(values.shape[0])]
        filled = values.shape[0] * values.shape[1]
        rows.append(jnp.concatenate(pieces + [jnp.zeros((1, width - filled), F32)], 1))
    rows.append(jnp.zeros((SMALL_ROWS - len(rows), width), F32))
    vectors = jnp.concatenate(rows, 0).astype(BF16)
    for target in outs[:3]:
        target[4 * part : start] = vectors


def forward_attention_kernel(
    groups, shards, me_ref, len_ref, tok_ref, *refs
):
    relative = not shards.stacked
    (first_sources,), refs = shards.sources(refs, groups, 0)
    (query_ref, key_ref, value_ref, probs_ref, normed_ref, scale_ref, vec_ref, mine_ref, other_ref,
     wq, wk, wv, wo, smalls, joined, turned, sems) = refs
    me = me_ref[0]
    rows, width = tok_ref.shape
    part = width // groups
    copies = load(me, first_sources, relative, [
        (0, part, wq, None), (part, part, wk, None), (2 * part, part, wv, None),
        (3 * part, part, wo, None), (4 * part, SMALL_ROWS, smalls, None)], sems, 0)
    for copy in copies:
        copy.start()
    tokens = tok_ref[...]
    ends = ends_of(len_ref, len_ref.shape[1])
    across = lax.broadcasted_iota(jnp.int32, (rows, rows), 1)
    down = lax.broadcasted_iota(jnp.int32, (rows, rows), 0)
    segment_across = jnp.zeros((rows, rows), jnp.int32)
    segment_down = jnp.zeros((rows, rows), jnp.int32)
    for end in ends:
        segment_across = segment_across + (across >= end).astype(jnp.int32)
        segment_down = segment_down + (down >= end).astype(jnp.int32)
    same = segment_across == segment_down
    turned[0] = tokens.astype(F32).T.astype(BF16).reshape(groups // 2, 2, part, rows)
    for copy in copies:
        copy.wait()
    ff_part = vec_ref.shape[1] // groups
    vec_ref[...] = jnp.zeros_like(vec_ref)
    for owner in range(groups):
        block = smalls[owner * SMALL_ROWS : (owner + 1) * SMALL_ROWS].astype(F32)
        for row in range(9):
            size = ff_part if row == 3 else part
            vec_ref[row : row + 1, owner * size : (owner + 1) * size] = block[row : row + 1, :size]
    query = (dot(tokens, wq[...]) + vec_ref[0:1, :width]).astype(BF16)
    keys = dot(tokens, wk[...]).astype(BF16)
    values = (dot(tokens, wv[...]) + vec_ref[1:2, :width]).astype(BF16)
    query_ref[...] = query
    key_ref[...] = keys
    value_ref[...] = values
    for head in range(HEADS):
        lanes = slice(head * HEAD_DIM, (head + 1) * HEAD_DIM)
        scores = dot_rt(query[:, lanes], keys[:, lanes]) * HEAD_DIM ** (-0.5)
        scores = jnp.where(same, scores, -1e30)
        raised = jnp.exp(scores - jnp.max(scores, -1, keepdims=True))
        probs = raised * (1.0 / jnp.sum(raised, -1, keepdims=True))
        probs_ref[head] = probs
        joined[:, lanes] = dot(probs.astype(BF16), values[:, lanes]).astype(BF16)
    attended = joined[...]
    summed = tokens.astype(F32) + dot(attended, wo[...]) + vec_ref[2:3, :width]
    normed, scale = normalize(summed)
    normed_ref[...] = normed
    scale_ref[...] = scale
    first_low = normed * vec_ref[5:6, :width] + vec_ref[6:7, :width]
    turned[1] = attended.astype(F32).T.astype(BF16).reshape(groups // 2, 2, part, rows)
    turned[2] = first_low.astype(BF16).astype(F32).T.astype(BF16).reshape(groups // 2, 2, part, rows)
    core = me & 1
    for kind in range(3):
        for block in range(groups // 2):
            mine_ref[kind, block] = turned[kind, block, core]
            other_ref[kind, block] = turned[kind, block, 1 - core]


def hidden_kernel(
    groups, shards, me_ref, len_ref, normed_ref, scale_ref, vec_ref, cot_ref, *refs
):
    relative = not shards.stacked
    (first_sources, inner_sources, outer_sources), refs = shards.sources(refs, groups, 0, 1, 2)
    (out_ref, low_ref, mine_ref, other_ref, hidden_ref, branch_ref, first_ref, att_ref, sums_ref, hidden_sum_ref,
     wi, wo, wb, slopes, kept, sems) = refs
    me = me_ref[0]
    rows, width = normed_ref.shape
    hidden = vec_ref.shape[1]
    part = width // groups
    ff_part = hidden // groups
    copies = load(me, inner_sources, relative, inner_pieces(part, wi), sems, 0)
    more = load(me, outer_sources, relative, [(0, ff_part, wo, None)], sems, len(copies))
    last = load(
        me, first_sources, relative, [(3 * part, part, wb, None)], sems, len(copies) + len(more))
    for copy in copies + more + last:
        copy.start()
    first_normed = normed_ref[...]
    first_out = first_normed * vec_ref[5:6, :width] + vec_ref[6:7, :width]
    for copy in copies:
        copy.wait()
    first_low = first_out.astype(BF16)
    core = me & 1
    for start in range(0, hidden, width):
        lanes = slice(start, start + width)
        inner = dot(first_low, wi[:, lanes]) + vec_ref[3:4, lanes]
        below = 0.5 * (1.0 + lax.erf(inner * 0.7071067811865476))
        slopes[:, lanes] = below + inner * jnp.exp(-0.5 * inner * inner) * 0.3989422804014327
        activated = (inner * below).astype(BF16)
        for owner in range(start // ff_part, (start + width) // ff_part):
            first = owner * ff_part - start
            kept[owner // 2, owner % 2] = activated[:, first : first + ff_part]
    for copy in more:
        copy.wait()
    second_sum = first_out + vec_ref[4:5, :width]
    for owner in range(groups):
        second_sum = second_sum + dot(
            kept[owner // 2, owner % 2], wo[owner * ff_part : (owner + 1) * ff_part])
    normed, scale = normalize(second_sum)
    valid = valid_rows(len_ref, rows)
    gain = vec_ref[7:8, :width]
    out_ref[...] = (valid * (normed * gain + vec_ref[8:9, :width])).astype(BF16)
    upstream = cot_ref[...].astype(F32) * valid
    grad = norm_back(upstream * gain, normed, scale)
    low = grad.astype(BF16)
    low_ref[...] = low
    sums_ref[0:1] = row_sum(low.astype(F32))
    sums_ref[1:2] = row_sum(upstream * normed)
    sums_ref[2:3] = row_sum(upstream)
    for block in range(groups // 2):
        mine_ref[block] = kept[block, core]
        other_ref[block] = kept[block, 1 - core]
    for start in range(0, hidden, width):
        lanes = slice(start, start + width)
        inner_low = (dot_rt(low, wo[lanes]) * slopes[:, lanes]).astype(BF16)
        hidden_ref[:, lanes] = inner_low
        hidden_sum_ref[:, lanes] = row_sum(inner_low.astype(F32))
    grad_out = grad + dot_rt(hidden_ref[...], wi[...])
    sums_ref[3:4] = row_sum(grad_out * first_normed)
    sums_ref[4:5] = row_sum(grad_out)
    grad_first = norm_back(grad_out * vec_ref[5:6, :width], first_normed, scale_ref[...])
    branch = grad_first.astype(BF16)
    sums_ref[5:6] = row_sum(branch.astype(F32))
    first_ref[...] = grad_first
    branch_ref[...] = branch
    for copy in last:
        copy.wait()
    att_ref[...] = dot_rt(branch, wb[...]).astype(BF16)


def backward_attention_kernel(
    groups, me_ref, query_ref, key_ref, value_ref, probs_ref, att_ref,
    sums, hidden_sums, grads_ref, mine_ref, other_ref, packed
):
    rows, width = query_ref.shape
    hidden = hidden_sums.shape[1]
    part = width // groups
    ff_part = hidden // groups
    for head in range(HEADS):
        lanes = slice(head * HEAD_DIM, (head + 1) * HEAD_DIM)
        grad_att = att_ref[:, lanes]
        probs = probs_ref[head]
        grad_probs = dot_rt(grad_att, value_ref[:, lanes])
        mixed = probs * grad_probs
        grad_scores = (mixed - probs * jnp.sum(mixed, -1, keepdims=True)).astype(BF16)
        scale = HEAD_DIM ** (-0.5)
        for kind, grad in enumerate((
            scale * dot(grad_scores, key_ref[:, lanes]),
            scale * dot_lt(grad_scores, query_ref[:, lanes]),
            dot_lt(probs.astype(BF16), grad_att),
        )):
            first = kind * width + head * HEAD_DIM
            grads_ref[:, first : first + HEAD_DIM] = grad.astype(BF16)
    packed[...] = jnp.zeros_like(packed)
    query_sum = row_sum(grads_ref[:, :width].astype(F32))
    value_sum = row_sum(grads_ref[:, 2 * width :].astype(F32))
    ordered = (
        query_sum, value_sum, sums[5:6], hidden_sums[0:1], sums[0:1],
        sums[3:4], sums[4:5], sums[1:2], sums[2:3])
    for owner in range(groups):
        for row, vector in enumerate(ordered):
            size = ff_part if row == 3 else part
            packed[owner // 2, owner % 2, row : row + 1, :size] = vector[
                :, owner * size : (owner + 1) * size]
    core = me_ref[0] & 1
    for block in range(groups // 2):
        mine_ref[block] = packed[block, core]
        other_ref[block] = packed[block, 1 - core].astype(BF16)


def grad_tokens_kernel(groups, shards, me_ref, grads_ref, first_ref, *refs):
    relative = not shards.stacked
    (first_sources,), refs = shards.sources(refs, groups, 0)
    out_ref, wq, wk, wv, sems = refs
    me = me_ref[0]
    rows, width = first_ref.shape
    part = width // groups
    copies = load(me, first_sources, relative, [
        (0, part, wq, None), (part, part, wk, None), (2 * part, part, wv, None)], sems, 0)
    for copy in copies:
        copy.start()
    for copy in copies:
        copy.wait()
    total = first_ref[...]
    for kind, weight in enumerate((wq, wk, wv)):
        total = total + dot_rt(grads_ref[:, kind * width : (kind + 1) * width], weight[...])
    out_ref[...] = total.astype(BF16)


def put(refs, blocks, slot, start, lanes, value):
    ref = refs[slot] if blocks == 4 else refs[0].at[slot]
    ref[start : start + value.shape[0], lanes] = value.astype(ref.dtype)


def outer_grad_kernel(blocks, me_ref, mine_ref, given_ref, low_ref, low_given_ref, *refs):
    first = me_ref[0] >> 1 if blocks == 4 else 0
    low = jnp.concatenate([low_ref[...], low_given_ref[...]], 0)
    for slot in range(blocks):
        block = slot ^ first
        acts = jnp.concatenate([mine_ref[block], given_ref[block]], 0)
        put(refs, blocks, slot, 0, slice(None), dot_lt(acts, low))


def inner_grad_kernel(blocks, me_ref, mine_ref, given_ref, low_ref, low_given_ref, *refs):
    first = me_ref[0] >> 1 if blocks == 4 else 0
    left = jnp.concatenate([
        jnp.concatenate([mine_ref[2, slot ^ first], given_ref[2, slot ^ first]], 1)
        for slot in range(blocks)], 0)
    part = left.shape[0] // blocks
    step = 512
    for start in range(0, low_ref.shape[1], step):
        lanes = slice(start, start + step)
        low = jnp.concatenate([low_ref[:, lanes], low_given_ref[:, lanes]], 0)
        grad = dot(left, low)
        for slot in range(blocks):
            put(refs, blocks, slot, 0, lanes, grad[slot * part : (slot + 1) * part])


def attention_grad_kernel(
    blocks, me_ref, mine_ref, given_ref, grads_ref, grads_given_ref, branch_ref, branch_given_ref,
    small_ref, small_given_ref, *refs
):
    first = me_ref[0] >> 1 if blocks == 4 else 0
    width = branch_ref.shape[1]
    lefts = [
        jnp.concatenate([
            jnp.concatenate([mine_ref[kind, slot ^ first], given_ref[kind, slot ^ first]], 1)
            for slot in range(blocks)], 0)
        for kind in range(2)]
    part = lefts[0].shape[0] // blocks
    for kind in range(4):
        if kind < 3:
            lanes = slice(kind * width, (kind + 1) * width)
            right = jnp.concatenate([grads_ref[:, lanes], grads_given_ref[:, lanes]], 0)
            grad = dot(lefts[0], right)
        else:
            grad = dot(lefts[1], jnp.concatenate([branch_ref[...], branch_given_ref[...]], 0))
        for slot in range(blocks):
            put(refs, blocks, slot, kind * part, slice(None), grad[slot * part : (slot + 1) * part])
    for slot in range(blocks):
        small = small_ref[slot ^ first] + small_given_ref[slot ^ first].astype(F32)
        put(refs, blocks, slot, 4 * part, slice(None), small)


ANY = pl.BlockSpec(memory_space=pl.ANY)
HBM = pl.BlockSpec(memory_space=pltpu.HBM)
VMEM = pl.BlockSpec(memory_space=pltpu.VMEM)
SMEM = pl.BlockSpec(memory_space=pltpu.SMEM)


def call(kernel, in_specs, outs, scratch, name):
    return pl.pallas_call(
        kernel,
        out_shape=[jax.ShapeDtypeStruct(shape, dtype) for shape, dtype in outs],
        in_specs=in_specs,
        out_specs=[VMEM] * len(outs),
        scratch_shapes=scratch,
        compiler_params=pltpu.CompilerParams(vmem_limit_bytes=VMEM_LIMIT),
        cost_estimate=pl.CostEstimate(flops=2_000_000_000, bytes_accessed=8_000_000, transcendentals=0),
        name=name,
    )


def after(value, *others):
    return lax.optimization_barrier((value,) + others)[0]


def flip(groups, mask):
    return [(index, index ^ mask) for index in range(groups)]


def swap(value, groups, mask):
    return lax.ppermute(value, "dp", flip(groups, mask))


def swapped(value, groups):
    return [value, swap(value, groups, 1)]


def group_sum(parts, groups, *others):
    keep = parts[0]
    got = [swap(sent, groups, mask) for mask, sent in zip((2, 4, 6), parts[1:])]
    got = lax.optimization_barrier(tuple(got) + others)[:3]
    return keep + got[0].astype(F32) + got[1].astype(F32) + got[2].astype(F32)


def group_sum_any(stacked, groups):
    core = lax.axis_index("dp") & 1
    blocks = groups // 2
    full = jnp.zeros((blocks, 2) + stacked.shape[1:], stacked.dtype)
    full = lax.dynamic_update_slice_in_dim(full, stacked[:, None], core, 1)
    full = full.reshape((groups,) + stacked.shape[1:])
    return lax.psum_scatter(full, "dp", scatter_dimension=0, tiled=False).astype(F32)


def copies_sum(value, *others):
    place = lax.axis_index("rep")
    size = value.shape[-1] // 4
    value = value.astype(BF16)

    def send(piece, mask):
        return lax.ppermute(piece, "rep", [(index, index ^ mask) for index in range(4)])

    quarters = [
        lax.dynamic_slice_in_dim(value, (place ^ mask) * size, size, value.ndim - 1)
        for mask in range(4)]
    total = quarters[0].astype(F32)
    for mask in (2, 3, 1):
        total = total + send(quarters[mask], mask).astype(F32)
    total = total.astype(BF16)
    gathered = tuple(send(total, mask) for mask in (1, 2, 3))
    one, two, three = lax.optimization_barrier(gathered + others)[:3]
    odd = (place & 1) == 1
    high = (place & 2) == 2
    lower = (jnp.where(odd, one, total), jnp.where(odd, total, one))
    upper = (jnp.where(odd, three, two), jnp.where(odd, two, three))
    pieces = [jnp.where(high, second, first) for first, second in zip(lower, upper)]
    pieces += [jnp.where(high, first, second) for first, second in zip(lower, upper)]
    return jnp.concatenate(pieces, -1).astype(F32)


class CopiesSum:
    near = [(0, 1), (1, 0), (2, 3), (3, 2)]
    far = [(0, 2), (2, 0), (1, 3), (3, 1)]

    def __init__(self, value):
        self.value = value.astype(BF16)
        self.upper = lax.axis_index("rep") & 1
        self.half = value.shape[0] // 2

    def start(self, *others):
        value = after(self.value, *others)
        self.kept = lax.dynamic_slice_in_dim(value, self.upper * self.half, self.half)
        sent = lax.dynamic_slice_in_dim(value, (1 - self.upper) * self.half, self.half)
        self.got = lax.ppermute(sent, "rep", self.near)

    def cross(self, *others):
        got = after(self.got, *others)
        self.pair = (self.kept.astype(F32) + got.astype(F32)).astype(BF16)
        self.got = lax.ppermute(self.pair, "rep", self.far)
        return self.pair

    def back(self, *others):
        got = after(self.got, *others)
        self.total = (self.pair.astype(F32) + got.astype(F32)).astype(BF16)
        self.got = lax.ppermute(self.total, "rep", self.near)
        return self.total

    def results(self, *columns):
        lower = self.upper == 0
        found = []
        for start, end in columns:
            total, got = self.total[:, start:end], self.got[:, start:end]
            halves = [jnp.where(lower, total, got), jnp.where(lower, got, total)]
            found.append(jnp.concatenate(halves).astype(F32))
        return found


def local(
    tokens,
    cotangent,
    seq_lengths,
    query_weight,
    key_weight,
    value_weight,
    output_weight,
    inner_weight,
    outer_weight,
    query_bias,
    value_bias,
    output_bias,
    inner_bias,
    outer_bias,
    first_gain,
    first_shift,
    second_gain,
    second_shift,
):
    groups = lax.axis_size("dp")
    blocks = groups // 2
    rows, width = tokens.shape
    part = width // groups
    ff_part = outer_weight.shape[0]
    hidden = ff_part * groups
    me = lax.axis_index("dp").astype(jnp.int32).reshape(1)
    smalls = (
        query_bias,
        value_bias,
        output_bias,
        inner_bias,
        outer_bias,
        first_gain,
        first_shift,
        second_gain,
        second_shift,
    )
    small_inputs = [
        piece.reshape(max(1, piece.shape[0] // 128), min(128, piece.shape[0])) for piece in smalls]
    first_rows = 4 * part + SMALL_ROWS
    inner_rows = hidden // width * part
    first_own, with_inner, with_outer, inner_own = call(
        functools.partial(pack_kernel, len(smalls)),
        [HBM] * (6 + len(smalls)),
        [((first_rows, width), BF16), ((first_rows + inner_rows, width), BF16),
         ((first_rows + ff_part, width), BF16), ((inner_rows, width), BF16)],
        [pltpu.VMEM(piece.shape, BF16) for piece in small_inputs]
        + [pltpu.SemaphoreType.DMA((13 + 2 * hidden // width + len(smalls),))],
        "pack",
    )(query_weight, key_weight, value_weight, output_weight, *small_inputs,
      inner_weight, outer_weight)
    if groups == 8:
        inner_y = swap(inner_own, groups, 4)
        outer_x = swap(after(outer_weight, first_own), groups, 2)
        over_x, over_y = swap(with_inner, groups, 2), swap(with_outer, groups, 4)
        far_first = swap(first_own, groups, 6)
        far_inner, far_outer = swap(inner_y, groups, 2), swap(outer_x, groups, 4)
        hops = lax.optimization_barrier((over_x, over_y, far_first, inner_y, outer_x))
        arrays = []
        for value in (with_inner, outer_weight) + hops:
            arrays.extend(swapped(value, groups))
        at = first_rows

        def spread(*found):
            return [(2 * index + core, row) for index, row in found for core in range(2)]

        shards = Shards(arrays, (
            spread((0, 0), (2, 0), (3, 0), (4, 0)),
            spread((0, at), (2, at), (5, 0), (7, 0)),
            spread((1, 0), (6, 0), (3, at), (8, 0))), False)
    else:
        packed = jnp.concatenate([with_inner, outer_weight])
        shards = Shards([lax.all_gather(packed, "dp", axis=0, tiled=False)],
                        (0, first_rows, first_rows + inner_rows), True)
    weight = (width, width)
    turned = (3, blocks, part, rows)
    query, keys, values, probs, normed, scale, vectors, mine, other = call(
        functools.partial(forward_attention_kernel, groups, shards),
        [SMEM, SMEM, VMEM] + [ANY] * len(shards.operands(0)),
        [((rows, width), BF16)] * 3
        + [((HEADS, rows, rows), F32), ((rows, width), F32), ((rows, 1), F32),
           ((SMALL_ROWS, hidden), F32), (turned, BF16), (turned, BF16)],
        [pltpu.VMEM(weight, BF16)] * 4
        + [pltpu.VMEM((groups * SMALL_ROWS, width), BF16), pltpu.VMEM((rows, width), BF16),
           pltpu.VMEM((3, blocks, 2, part, rows), BF16), pltpu.SemaphoreType.DMA((5 * groups,))],
        "forward_attention",
    )(me, seq_lengths, tokens, *shards.operands(0))
    given = swap(other, groups, 1)
    if groups == 8:
        for value in lax.optimization_barrier((far_inner, far_outer, normed))[:2]:
            arrays.extend(swapped(value, groups))
    acts = (blocks, rows, ff_part)
    (layer_out, outer_low, act_mine, act_other, hidden_low, branch, grad_first, grad_att, sums,
     hidden_sums) = call(
        functools.partial(hidden_kernel, groups, shards),
        [SMEM, SMEM] + [VMEM] * 4 + [ANY] * len(shards.operands(0, 1, 2)),
        [((rows, width), BF16), ((rows, width), BF16), (acts, BF16), (acts, BF16),
         ((rows, hidden), BF16), ((rows, width), BF16), ((rows, width), F32), ((rows, width), BF16),
         ((8, width), F32), ((1, hidden), F32)],
        [pltpu.VMEM((width, hidden), BF16), pltpu.VMEM((hidden, width), BF16),
         pltpu.VMEM(weight, BF16), pltpu.VMEM((rows, hidden), F32),
         pltpu.VMEM((blocks, 2, rows, ff_part), BF16),
         pltpu.SemaphoreType.DMA(((2 + hidden // width) * groups,))],
        "hidden",
    )(me, seq_lengths, normed, scale, vectors, cotangent, *shards.operands(0, 1, 2))
    act_given = swap(act_other, groups, 1)
    outer_given = swap(outer_low, groups, 1)

    def grad_call(kernel, specs, shape, name):
        if blocks == 4:
            outs = [(shape, F32)] + [(shape, BF16)] * 3
        else:
            outs = [((blocks,) + shape, BF16)]
        return call(functools.partial(kernel, blocks), specs, outs, [], name)

    outer_parts = grad_call(
        outer_grad_kernel, [SMEM] + [VMEM] * 4, (ff_part, width), "outer_grad",
    )(me, act_mine, act_given, outer_low, outer_given)
    hidden_given = swap(hidden_low, groups, 1)
    branch_given = swap(branch, groups, 1)
    small = (blocks, SMALL_ROWS, width)
    grads, small_mine, small_other = call(
        functools.partial(backward_attention_kernel, groups),
        [SMEM] + [VMEM] * 7,
        [((rows, 3 * width), BF16), (small, F32), (small, BF16)],
        [pltpu.VMEM((blocks, 2, SMALL_ROWS, width), F32)],
        "backward_attention",
    )(me, query, keys, values, probs, after(grad_att, outer_parts[0]), sums, hidden_sums)
    grads_given = swap(grads, groups, 1)
    small_given = swap(small_other, groups, 1)
    inner_parts = grad_call(
        inner_grad_kernel, [SMEM] + [VMEM] * 4, (part, hidden), "inner_grad",
    )(me, mine, given, after(hidden_low, grads), hidden_given)
    direct = groups == 8 and lax.axis_size("rep") == 4
    if direct:
        first_sum = group_sum(outer_parts, groups, inner_parts[0])
        first_copies = CopiesSum(first_sum)
        first_copies.start()
    waited = (first_copies.kept,) if direct else ()
    attention_parts = grad_call(
        attention_grad_kernel, [SMEM] + [VMEM] * 8,
        (4 * part + SMALL_ROWS, width), "attention_grad",
    )(me, after(mine, *waited), given, grads, grads_given, branch, branch_given, small_mine, small_given)
    if direct:
        first_pair = first_copies.cross(attention_parts[0])
        second_sum = group_sum(inner_parts, groups, first_pair)
        second_copies = CopiesSum(second_sum)
        second_copies.start()
        waited = (second_copies.kept,)
    (grad_tokens,) = call(
        functools.partial(grad_tokens_kernel, groups, shards),
        [SMEM, VMEM, VMEM] + [ANY] * len(shards.operands(0)),
        [((rows, width), BF16)],
        [pltpu.VMEM(weight, BF16)] * 3 + [pltpu.SemaphoreType.DMA((3 * groups,))],
        "grad_tokens",
    )(me, after(grads, *waited), grad_first, *shards.operands(0))

    if direct:
        first_total = first_copies.back(grad_tokens)
        second_pair = second_copies.cross(first_total)
        third_sum = group_sum(attention_parts, groups, second_pair)
        second_copies.back(third_sum)
        (grad_outer,) = first_copies.results((0, width))
        (grad_inner,) = second_copies.results((0, hidden))
        grad_attention = copies_sum(third_sum, grad_outer, grad_inner)
    else:
        grad_outer, grad_inner, grad_attention = [
            lax.psum(group_sum_any(piece[0], groups).astype(BF16), "rep").astype(F32)
            for piece in (outer_parts, inner_parts, attention_parts)]
    return (
        layer_out,
        grad_tokens,
        grad_attention[:part],
        grad_attention[part : 2 * part],
        grad_attention[2 * part : 3 * part],
        grad_attention[3 * part : 4 * part],
        grad_inner,
        grad_outer,
    ) + tuple(grad_attention[4 * part + row, : piece.shape[0]] for row, piece in enumerate(smalls))


def solution(mesh):
    split = P(("dp", "rep"), None)
    rows = P("dp", None)
    vector = P("dp")
    return jax.shard_map(
        local,
        mesh=mesh,
        in_specs=(split,) * 3 + (rows,) * 6 + (vector,) * 9,
        out_specs=(split,) * 2 + (rows,) * 6 + (vector,) * 9,
        check_vma=False,
    )
```

```python
import functools

import jax
import jax.numpy as jnp
from jax import lax
from jax.experimental import pallas as pl
from jax.experimental.pallas import tpu as pltpu
from jax.sharding import PartitionSpec as P

HEADS = 8
HEAD_DIM = 64
EPS = 1e-05
SMALL_ROWS = 16
BF16 = jnp.bfloat16
F32 = jnp.float32
VMEM_LIMIT = 56 * 1024 * 1024


def dot(left, right):
    return lax.dot_general(left, right, (((1,), (0,)), ((), ())), preferred_element_type=F32)


def dot_rt(left, right):
    return lax.dot_general(left, right, (((1,), (1,)), ((), ())), preferred_element_type=F32)


def dot_lt(left, right):
    return lax.dot_general(left, right, (((0,), (0,)), ((), ())), preferred_element_type=F32)


def mean_of(values):
    return jnp.mean(values, -1, keepdims=True)


def normalize(summed):
    centred = summed - mean_of(summed)
    scale = lax.rsqrt(mean_of(centred * centred) + EPS)
    return centred * scale, scale


def norm_back(grad_normed, normed, scale):
    return scale * (grad_normed - mean_of(grad_normed) - normed * mean_of(grad_normed * normed))


def row_sum(values):
    return jnp.sum(values, 0, keepdims=True)


class Shards:
    def __init__(self, arrays, places, stacked):
        self.arrays = arrays
        self.places = places
        self.stacked = stacked

    def used(self, kinds):
        if self.stacked:
            return [0]
        return sorted({index for kind in kinds for index, _ in self.places[kind]})

    def operands(self, *kinds):
        return [self.arrays[index] for index in self.used(kinds)]

    def sources(self, refs, groups, *kinds):
        used = self.used(kinds)
        if self.stacked:
            return [[(refs[0].at[index], self.places[kind]) for index in range(groups)]
                    for kind in kinds], refs[1:]
        found = dict(zip(used, refs))
        return [[(found[index], row) for index, row in self.places[kind]]
                for kind in kinds], refs[len(used) :]


def load(me, sources, relative, pieces, sems, base):
    copies = []
    for index, (source, start) in enumerate(sources):
        owner = (me ^ index) if relative else index
        for first, size, target, column in pieces:
            place = owner * size
            if relative:
                place = pl.multiple_of(place, size)
            where = target.at[pl.ds(place, size)]
            if column is not None:
                where = target.at[pl.ds(place, size), pl.ds(*column)]
            if isinstance(start, tuple):
                chosen = source.at[pl.ds(start[0], size), pl.ds(*column)]
            else:
                chosen = source.at[pl.ds(start + first, size)]
            copies.append(pltpu.make_async_copy(chosen, where, sems.at[base + len(copies)]))
    return copies


def inner_pieces(part, wi):
    width = wi.shape[0]
    return [(index * part, part, wi, (index * width, width))
            for index in range(wi.shape[1] // width)]


def ends_of(len_ref, slots):
    ends = []
    total = jnp.int32(0)
    for slot in range(slots):
        total = total + len_ref[0, slot]
        ends.append(total)
    return ends


def valid_rows(len_ref, rows):
    ends = ends_of(len_ref, len_ref.shape[1])
    places = lax.broadcasted_iota(jnp.int32, (rows, 1), 0)
    return (places < ends[-1]).astype(F32)


def pack_kernel(count, *refs):
    sources = refs[: 4 + count]
    first_ref = refs[4 + count]
    small_refs = refs[5 + count : -1]
    sems = refs[-1]
    part, width = sources[0].shape
    pairs = [(source, first_ref.at[pl.ds(index * part, part)])
             for index, source in enumerate(sources[:4])]
    pairs += list(zip(sources[4:], small_refs))
    copies = [
        pltpu.make_async_copy(source, target, sems.at[index])
        for index, (source, target) in enumerate(pairs)]
    for copy in copies:
        copy.start()
    for copy in copies:
        copy.wait()
    rows = []
    for small in small_refs:
        values = small[...].astype(F32)
        pieces = [values[row : row + 1] for row in range(values.shape[0])]
        filled = values.shape[0] * values.shape[1]
        rows.append(jnp.concatenate(pieces + [jnp.zeros((1, width - filled), F32)], 1))
    rows.append(jnp.zeros((SMALL_ROWS - len(rows), width), F32))
    first_ref[4 * part :] = jnp.concatenate(rows, 0).astype(BF16)


def forward_attention_kernel(
    groups, shards, me_ref, len_ref, tok_any, *refs
):
    relative = not shards.stacked
    (first_sources,), refs = shards.sources(refs, groups, 0)
    (query_ref, key_ref, value_ref, probs_ref, normed_ref, scale_ref, vec_ref, mine_ref, other_ref,
     wq, wk, wv, wo, smalls, joined, turned, tok_ref, sems) = refs
    me = me_ref[0]
    rows, width = tok_ref.shape
    part = width // groups
    copies = load(me, first_sources, relative, [
        (0, part, wq, None), (part, part, wk, None), (2 * part, part, wv, None),
        (3 * part, part, wo, None), (4 * part, SMALL_ROWS, smalls, None)], sems, 0)
    fetch = pltpu.make_async_copy(tok_any, tok_ref, sems.at[len(copies)])
    fetch.start()
    for kind in (4, 0, 1, 2, 3):
        for copy in copies[kind::5]:
            copy.start()
    fetch.wait()
    tokens = tok_ref[...]
    ends = ends_of(len_ref, len_ref.shape[1])
    across = lax.broadcasted_iota(jnp.int32, (rows, rows), 1)
    down = lax.broadcasted_iota(jnp.int32, (rows, rows), 0)
    segment_across = jnp.zeros((rows, rows), jnp.int32)
    segment_down = jnp.zeros((rows, rows), jnp.int32)
    for end in ends:
        segment_across = segment_across + (across >= end).astype(jnp.int32)
        segment_down = segment_down + (down >= end).astype(jnp.int32)
    same = segment_across == segment_down
    turned[0] = tokens.astype(F32).T.astype(BF16).reshape(groups // 2, 2, part, rows)
    for copy in copies[4::5] + copies[0::5]:
        copy.wait()
    ff_part = vec_ref.shape[1] // groups
    vec_ref[...] = jnp.zeros_like(vec_ref)
    for owner in range(groups):
        block = smalls[owner * SMALL_ROWS : (owner + 1) * SMALL_ROWS].astype(F32)
        for row in range(9):
            size = ff_part if row == 3 else part
            vec_ref[row : row + 1, owner * size : (owner + 1) * size] = block[row : row + 1, :size]
    query = (dot(tokens, wq[...]) + vec_ref[0:1, :width]).astype(BF16)
    for copy in copies[1::5]:
        copy.wait()
    keys = dot(tokens, wk[...]).astype(BF16)
    for copy in copies[2::5]:
        copy.wait()
    values = (dot(tokens, wv[...]) + vec_ref[1:2, :width]).astype(BF16)
    query_ref[...] = query
    key_ref[...] = keys
    value_ref[...] = values
    for head in range(HEADS):
        lanes = slice(head * HEAD_DIM, (head + 1) * HEAD_DIM)
        scores = dot_rt(keys[:, lanes], query[:, lanes]) * HEAD_DIM ** (-0.5)
        scores = jnp.where(same, scores, -1e30)
        raised = jnp.exp(scores - jnp.max(scores, 0, keepdims=True))
        probs = (raised * (1.0 / jnp.sum(raised, 0, keepdims=True))).astype(BF16)
        probs_ref[head] = probs
        joined[:, lanes] = dot_lt(probs, values[:, lanes]).astype(BF16)
    for copy in copies[3::5]:
        copy.wait()
    attended = joined[...]
    summed = tokens.astype(F32) + dot(attended, wo[...]) + vec_ref[2:3, :width]
    normed, scale = normalize(summed)
    normed_ref[...] = normed
    scale_ref[...] = scale
    first_low = normed * vec_ref[5:6, :width] + vec_ref[6:7, :width]
    turned[1] = attended.astype(F32).T.astype(BF16).reshape(groups // 2, 2, part, rows)
    turned[2] = first_low.astype(BF16).astype(F32).T.astype(BF16).reshape(groups // 2, 2, part, rows)
    core = me & 1
    for kind in range(3):
        for block in range(groups // 2):
            mine_ref[kind, block] = turned[kind, block, core]
            other_ref[kind, block] = turned[kind, block, 1 - core]


def hidden_kernel(
    groups, shards, me_ref, len_ref, normed_any, scale_any, vec_any, cot_any, *refs
):
    relative = not shards.stacked
    (first_sources, inner_sources, outer_sources), refs = shards.sources(refs, groups, 0, 1, 2)
    (out_ref, low_ref, mine_ref, other_ref, hidden_ref, branch_ref, first_ref, att_ref, sums_ref, hidden_sum_ref,
     wi, wo, wb, slopes, kept, normed_ref, scale_ref, vec_ref, cot_ref, sems) = refs
    me = me_ref[0]
    rows, width = normed_ref.shape
    hidden = vec_ref.shape[1]
    part = width // groups
    ff_part = hidden // groups
    copies = load(me, inner_sources, relative, inner_pieces(part, wi), sems, 0)
    more = load(me, outer_sources, relative, [(0, ff_part, wo, None)], sems, len(copies))
    last = load(
        me, first_sources, relative, [(3 * part, part, wb, None)], sems, len(copies) + len(more))
    count = len(copies) + len(more) + len(last)
    inputs = [
        pltpu.make_async_copy(source, target, sems.at[count + index])
        for index, (source, target) in enumerate((
            (normed_any, normed_ref), (vec_any, vec_ref), (scale_any, scale_ref),
            (cot_any, cot_ref)))]
    for copy in inputs:
        copy.start()
    for chunk in range(hidden // width):
        for copy in copies[chunk :: hidden // width]:
            copy.start()
    for copy in more + last:
        copy.start()
    for copy in inputs:
        copy.wait()
    first_normed = normed_ref[...]
    first_out = first_normed * vec_ref[5:6, :width] + vec_ref[6:7, :width]
    first_low = first_out.astype(BF16)
    core = me & 1
    for start in range(0, hidden, width):
        lanes = slice(start, start + width)
        for copy in copies[start // width :: hidden // width]:
            copy.wait()
        inner = dot(first_low, wi[:, lanes]) + vec_ref[3:4, lanes]
        below = 0.5 * (1.0 + lax.erf(inner * 0.7071067811865476))
        slopes[:, lanes] = below + inner * jnp.exp(-0.5 * inner * inner) * 0.3989422804014327
        activated = (inner * below).astype(BF16)
        for owner in range(start // ff_part, (start + width) // ff_part):
            first = owner * ff_part - start
            kept[owner // 2, owner % 2] = activated[:, first : first + ff_part]
    for copy in more:
        copy.wait()
    second_sum = first_out + vec_ref[4:5, :width]
    for owner in range(groups):
        second_sum = second_sum + dot(
            kept[owner // 2, owner % 2], wo[owner * ff_part : (owner + 1) * ff_part])
    normed, scale = normalize(second_sum)
    valid = valid_rows(len_ref, rows)
    gain = vec_ref[7:8, :width]
    out_ref[...] = (valid * (normed * gain + vec_ref[8:9, :width])).astype(BF16)
    upstream = cot_ref[...].astype(F32) * valid
    grad = norm_back(upstream * gain, normed, scale)
    low = grad.astype(BF16)
    low_ref[...] = low
    sums_ref[0:1] = row_sum(low.astype(F32))
    sums_ref[1:2] = row_sum(upstream * normed)
    sums_ref[2:3] = row_sum(upstream)
    for block in range(groups // 2):
        mine_ref[block] = kept[block, core]
        other_ref[block] = kept[block, 1 - core]
    for start in range(0, hidden, width):
        lanes = slice(start, start + width)
        inner_low = (dot_rt(low, wo[lanes]) * slopes[:, lanes]).astype(BF16)
        hidden_ref[:, lanes] = inner_low
        hidden_sum_ref[:, lanes] = row_sum(inner_low.astype(F32))
    grad_out = grad + dot_rt(hidden_ref[...], wi[...])
    sums_ref[3:4] = row_sum(grad_out * first_normed)
    sums_ref[4:5] = row_sum(grad_out)
    grad_first = norm_back(grad_out * vec_ref[5:6, :width], first_normed, scale_ref[...])
    branch = grad_first.astype(BF16)
    sums_ref[5:6] = row_sum(branch.astype(F32))
    first_ref[...] = grad_first
    branch_ref[...] = branch
    for copy in last:
        copy.wait()
    att_ref[...] = dot_rt(branch, wb[...]).astype(BF16)


def backward_attention_kernel(
    groups, me_ref, query_ref, key_ref, value_ref, probs_ref, att_ref,
    sums, hidden_sums, grads_ref, mine_ref, other_ref, packed
):
    rows, width = query_ref.shape
    hidden = hidden_sums.shape[1]
    part = width // groups
    ff_part = hidden // groups
    for head in range(HEADS):
        lanes = slice(head * HEAD_DIM, (head + 1) * HEAD_DIM)
        grad_att = att_ref[:, lanes]
        probs = probs_ref[head].astype(F32)
        grad_probs = dot_rt(value_ref[:, lanes], grad_att)
        mixed = probs * grad_probs
        grad_scores = (mixed - probs * jnp.sum(mixed, 0, keepdims=True)).astype(BF16)
        scale = HEAD_DIM ** (-0.5)
        for kind, grad in enumerate((
            scale * dot_lt(grad_scores, key_ref[:, lanes]),
            scale * dot(grad_scores, query_ref[:, lanes]),
            dot(probs_ref[head], grad_att),
        )):
            first = kind * width + head * HEAD_DIM
            grads_ref[:, first : first + HEAD_DIM] = grad.astype(BF16)
    packed[...] = jnp.zeros_like(packed)
    query_sum = row_sum(grads_ref[:, :width].astype(F32))
    value_sum = row_sum(grads_ref[:, 2 * width :].astype(F32))
    ordered = (
        query_sum, value_sum, sums[5:6], hidden_sums[0:1], sums[0:1],
        sums[3:4], sums[4:5], sums[1:2], sums[2:3])
    for owner in range(groups):
        for row, vector in enumerate(ordered):
            size = ff_part if row == 3 else part
            packed[owner // 2, owner % 2, row : row + 1, :size] = vector[
                :, owner * size : (owner + 1) * size]
    core = me_ref[0] & 1
    for block in range(groups // 2):
        mine_ref[block] = packed[block, core]
        other_ref[block] = packed[block, 1 - core].astype(BF16)


def grad_tokens_kernel(groups, shards, me_ref, grads_ref, first_ref, *refs):
    relative = not shards.stacked
    (first_sources,), refs = shards.sources(refs, groups, 0)
    out_ref, wq, wk, wv, sems = refs
    me = me_ref[0]
    rows, width = first_ref.shape
    part = width // groups
    copies = load(me, first_sources, relative, [
        (0, part, wq, None), (part, part, wk, None), (2 * part, part, wv, None)], sems, 0)
    for copy in copies:
        copy.start()
    for copy in copies:
        copy.wait()
    total = first_ref[...]
    for kind, weight in enumerate((wq, wk, wv)):
        total = total + dot_rt(grads_ref[:, kind * width : (kind + 1) * width], weight[...])
    out_ref[...] = total.astype(BF16)


def put(refs, blocks, slot, start, lanes, value):
    ref = refs[slot] if blocks == 4 else refs[0].at[slot]
    ref[start : start + value.shape[0], lanes] = value.astype(ref.dtype)


def outer_grad_kernel(blocks, me_ref, mine_ref, given_ref, low_ref, low_given_ref, *refs):
    first = me_ref[0] >> 1 if blocks == 4 else 0
    low = jnp.concatenate([low_ref[...], low_given_ref[...]], 0)
    for slot in range(blocks):
        block = slot ^ first
        acts = jnp.concatenate([mine_ref[block], given_ref[block]], 0)
        put(refs, blocks, slot, 0, slice(None), dot_lt(acts, low))


def inner_grad_kernel(blocks, me_ref, mine_ref, given_ref, low_ref, low_given_ref, *refs):
    first = me_ref[0] >> 1 if blocks == 4 else 0
    left = jnp.concatenate([
        jnp.concatenate([mine_ref[2, slot ^ first], given_ref[2, slot ^ first]], 1)
        for slot in range(blocks)], 0)
    part = left.shape[0] // blocks
    step = 512
    for start in range(0, low_ref.shape[1], step):
        lanes = slice(start, start + step)
        low = jnp.concatenate([low_ref[:, lanes], low_given_ref[:, lanes]], 0)
        grad = dot(left, low)
        for slot in range(blocks):
            put(refs, blocks, slot, 0, lanes, grad[slot * part : (slot + 1) * part])


def attention_grad_kernel(
    blocks, me_ref, mine_ref, given_ref, grads_ref, grads_given_ref, branch_ref, branch_given_ref,
    small_ref, small_given_ref, *refs
):
    first = me_ref[0] >> 1 if blocks == 4 else 0
    width = branch_ref.shape[1]
    lefts = [
        jnp.concatenate([
            jnp.concatenate([mine_ref[kind, slot ^ first], given_ref[kind, slot ^ first]], 1)
            for slot in range(blocks)], 0)
        for kind in range(2)]
    part = lefts[0].shape[0] // blocks
    for kind in range(4):
        if kind < 3:
            lanes = slice(kind * width, (kind + 1) * width)
            right = jnp.concatenate([grads_ref[:, lanes], grads_given_ref[:, lanes]], 0)
            grad = dot(lefts[0], right)
        else:
            grad = dot(lefts[1], jnp.concatenate([branch_ref[...], branch_given_ref[...]], 0))
        for slot in range(blocks):
            put(refs, blocks, slot, kind * part, slice(None), grad[slot * part : (slot + 1) * part])
    for slot in range(blocks):
        small = small_ref[slot ^ first] + small_given_ref[slot ^ first].astype(F32)
        put(refs, blocks, slot, 4 * part, slice(None), small)


ANY = pl.BlockSpec(memory_space=pl.ANY)
HBM = pl.BlockSpec(memory_space=pltpu.HBM)
VMEM = pl.BlockSpec(memory_space=pltpu.VMEM)
SMEM = pl.BlockSpec(memory_space=pltpu.SMEM)


def call(kernel, in_specs, outs, scratch, name):
    return pl.pallas_call(
        kernel,
        out_shape=[jax.ShapeDtypeStruct(shape, dtype) for shape, dtype in outs],
        in_specs=in_specs,
        out_specs=[VMEM] * len(outs),
        scratch_shapes=scratch,
        compiler_params=pltpu.CompilerParams(vmem_limit_bytes=VMEM_LIMIT),
        cost_estimate=pl.CostEstimate(flops=2_000_000_000, bytes_accessed=8_000_000, transcendentals=0),
        name=name,
    )


def after(value, *others):
    return lax.optimization_barrier((value,) + others)[0]


def flip(groups, mask):
    return [(index, index ^ mask) for index in range(groups)]


def swap(value, groups, mask):
    return lax.ppermute(value, "dp", flip(groups, mask))


def swapped(value, groups):
    return [value, swap(value, groups, 1)]


def group_sum(parts, groups, *others):
    keep = parts[0]
    got = [swap(sent, groups, mask) for mask, sent in zip((2, 4, 6), parts[1:])]
    got = lax.optimization_barrier(tuple(got) + others)[:3]
    return keep.astype(F32) + got[0].astype(F32) + got[1].astype(F32) + got[2].astype(F32)


def group_sum_any(stacked, groups):
    core = lax.axis_index("dp") & 1
    blocks = groups // 2
    full = jnp.zeros((blocks, 2) + stacked.shape[1:], stacked.dtype)
    full = lax.dynamic_update_slice_in_dim(full, stacked[:, None], core, 1)
    full = full.reshape((groups,) + stacked.shape[1:])
    return lax.psum_scatter(full, "dp", scatter_dimension=0, tiled=False).astype(F32)


def copies_sum(value, *others):
    place = lax.axis_index("rep")
    size = value.shape[-1] // 4
    value = value.astype(BF16)

    def send(piece, mask):
        return lax.ppermute(piece, "rep", [(index, index ^ mask) for index in range(4)])

    quarters = [
        lax.dynamic_slice_in_dim(value, (place ^ mask) * size, size, value.ndim - 1)
        for mask in range(4)]
    total = quarters[0].astype(F32)
    for mask in (2, 3, 1):
        total = total + send(quarters[mask], mask).astype(F32)
    total = total.astype(BF16)
    gathered = tuple(send(total, mask) for mask in (1, 2, 3))
    one, two, three = lax.optimization_barrier(gathered + others)[:3]
    odd = (place & 1) == 1
    high = (place & 2) == 2
    lower = (jnp.where(odd, one, total), jnp.where(odd, total, one))
    upper = (jnp.where(odd, three, two), jnp.where(odd, two, three))
    pieces = [jnp.where(high, second, first) for first, second in zip(lower, upper)]
    pieces += [jnp.where(high, first, second) for first, second in zip(lower, upper)]
    return jnp.concatenate(pieces, -1).astype(F32)


class CopiesSum:
    near = [(0, 1), (1, 0), (2, 3), (3, 2)]
    far = [(0, 2), (2, 0), (1, 3), (3, 1)]

    def __init__(self, value):
        self.value = value.astype(BF16)
        self.upper = lax.axis_index("rep") & 1
        self.half = value.shape[0] // 2

    def start(self, *others):
        value = after(self.value, *others)
        self.kept = lax.dynamic_slice_in_dim(value, self.upper * self.half, self.half)
        sent = lax.dynamic_slice_in_dim(value, (1 - self.upper) * self.half, self.half)
        self.got = lax.ppermute(sent, "rep", self.near)

    def cross(self, *others):
        got = after(self.got, *others)
        self.pair = (self.kept.astype(F32) + got.astype(F32)).astype(BF16)
        self.got = lax.ppermute(self.pair, "rep", self.far)
        return self.pair

    def back(self, *others):
        got = after(self.got, *others)
        self.total = (self.pair.astype(F32) + got.astype(F32)).astype(BF16)
        self.got = lax.ppermute(self.total, "rep", self.near)
        return self.total

    def results(self, *columns):
        lower = self.upper == 0
        found = []
        for start, end in columns:
            total, got = self.total[:, start:end], self.got[:, start:end]
            halves = [jnp.where(lower, total, got), jnp.where(lower, got, total)]
            found.append(jnp.concatenate(halves).astype(F32))
        return found


def local(
    tokens,
    cotangent,
    seq_lengths,
    query_weight,
    key_weight,
    value_weight,
    output_weight,
    inner_weight,
    outer_weight,
    query_bias,
    value_bias,
    output_bias,
    inner_bias,
    outer_bias,
    first_gain,
    first_shift,
    second_gain,
    second_shift,
):
    groups = lax.axis_size("dp")
    blocks = groups // 2
    rows, width = tokens.shape
    part = width // groups
    ff_part = outer_weight.shape[0]
    hidden = ff_part * groups
    me = lax.axis_index("dp").astype(jnp.int32).reshape(1)
    smalls = (
        query_bias,
        value_bias,
        output_bias,
        inner_bias,
        outer_bias,
        first_gain,
        first_shift,
        second_gain,
        second_shift,
    )
    small_inputs = [
        piece.reshape(max(1, piece.shape[0] // 128), min(128, piece.shape[0])) for piece in smalls]
    first_rows = 4 * part + SMALL_ROWS
    (first_own,) = call(
        functools.partial(pack_kernel, len(smalls)),
        [HBM] * (4 + len(smalls)),
        [((first_rows, width), BF16)],
        [pltpu.VMEM(piece.shape, BF16) for piece in small_inputs]
        + [pltpu.SemaphoreType.DMA((4 + len(smalls),))],
        "pack",
    )(query_weight, key_weight, value_weight, output_weight, *small_inputs)
    if groups == 8:
        inner_y = swap(inner_weight, groups, 4)
        outer_x = swap(outer_weight, groups, 2)
        first_hops = [swap(first_own, groups, mask) for mask in (6, 2, 4)]
        own = (first_own, inner_weight, outer_weight)
        *hops, first_pair, inner_pair, outer_pair = lax.optimization_barrier(
            (*first_hops, inner_y, outer_x) + tuple(swap(value, groups, 1) for value in own))
        inner_x = swap(jnp.concatenate([inner_weight, hops[3]]), groups, 2)
        outer_y = swap(jnp.concatenate([outer_weight, hops[4]]), groups, 4)
        arrays = [first_own, first_pair, inner_weight, inner_pair, outer_weight, outer_pair]
        for value in hops:
            arrays.extend(swapped(value, groups))

        def spread(*found):
            return [(2 * index + core, row) for index, row in found for core in range(2)]

        shards = Shards(arrays, (
            spread((0, 0), (4, 0), (5, 0), (3, 0)),
            spread((1, (0,)), (8, (0,)), (6, (0,)), (8, (part,))),
            spread((2, 0), (7, 0), (9, 0), (9, ff_part))), False)
    else:
        blocked = inner_weight.reshape(part, hidden // width, width).swapaxes(0, 1)
        packed = jnp.concatenate([first_own, blocked.reshape(-1, width), outer_weight])
        shards = Shards([lax.all_gather(packed, "dp", axis=0, tiled=False)],
                        (0, first_rows, packed.shape[0] - ff_part), True)
    weight = (width, width)
    turned = (3, blocks, part, rows)
    query, keys, values, probs, normed, scale, vectors, mine, other = call(
        functools.partial(forward_attention_kernel, groups, shards),
        [SMEM, SMEM] + [ANY] * (1 + len(shards.operands(0))),
        [((rows, width), BF16)] * 3
        + [((HEADS, rows, rows), BF16), ((rows, width), F32), ((rows, 1), F32),
           ((SMALL_ROWS, hidden), F32), (turned, BF16), (turned, BF16)],
        [pltpu.VMEM(weight, BF16)] * 4
        + [pltpu.VMEM((groups * SMALL_ROWS, width), BF16), pltpu.VMEM((rows, width), BF16),
           pltpu.VMEM((3, blocks, 2, part, rows), BF16), pltpu.VMEM((rows, width), BF16),
           pltpu.SemaphoreType.DMA((5 * groups + 1,))],
        "forward_attention",
    )(me, seq_lengths, tokens, *shards.operands(0))
    given = swap(other, groups, 1)
    if groups == 8:
        inner_x, outer_y, arrays[13], arrays[15] = lax.optimization_barrier(
            (inner_x, outer_y, arrays[13], arrays[15], normed))[:4]
        for value in (inner_x, outer_y):
            arrays.extend(swapped(value, groups))
    acts = (blocks, rows, ff_part)
    (layer_out, outer_low, act_mine, act_other, hidden_low, branch, grad_first, grad_att, sums,
     hidden_sums) = call(
        functools.partial(hidden_kernel, groups, shards),
        [SMEM, SMEM] + [ANY] * (4 + len(shards.operands(0, 1, 2))),
        [((rows, width), BF16), ((rows, width), BF16), (acts, BF16), (acts, BF16),
         ((rows, hidden), BF16), ((rows, width), BF16), ((rows, width), F32), ((rows, width), BF16),
         ((8, width), F32), ((1, hidden), F32)],
        [pltpu.VMEM((width, hidden), BF16), pltpu.VMEM((hidden, width), BF16),
         pltpu.VMEM(weight, BF16), pltpu.VMEM((rows, hidden), F32),
         pltpu.VMEM((blocks, 2, rows, ff_part), BF16),
         pltpu.VMEM((rows, width), F32), pltpu.VMEM((rows, 1), F32),
         pltpu.VMEM((SMALL_ROWS, hidden), F32), pltpu.VMEM((rows, width), BF16),
         pltpu.SemaphoreType.DMA(((2 + hidden // width) * groups + 4,))],
        "hidden",
    )(me, seq_lengths, normed, scale, vectors, cotangent, *shards.operands(0, 1, 2))
    act_given = swap(act_other, groups, 1)
    outer_given = swap(outer_low, groups, 1)

    def grad_call(kernel, specs, shape, name):
        if blocks == 4:
            outs = [(shape, BF16)] * 4
        else:
            outs = [((blocks,) + shape, BF16)]
        return call(functools.partial(kernel, blocks), specs, outs, [], name)

    outer_parts = grad_call(
        outer_grad_kernel, [SMEM] + [VMEM] * 4, (ff_part, width), "outer_grad",
    )(me, act_mine, act_given, outer_low, outer_given)
    hidden_given = swap(after(hidden_low, outer_parts[0]), groups, 1)
    branch_given = swap(after(branch, outer_parts[0]), groups, 1)
    small = (blocks, SMALL_ROWS, width)
    grads, small_mine, small_other = call(
        functools.partial(backward_attention_kernel, groups),
        [SMEM] + [VMEM] * 7,
        [((rows, 3 * width), BF16), (small, F32), (small, BF16)],
        [pltpu.VMEM((blocks, 2, SMALL_ROWS, width), F32)],
        "backward_attention",
    )(me, query, keys, values, probs, after(grad_att, outer_parts[0]), sums, hidden_sums)
    grads_given = swap(grads, groups, 1)
    small_given = swap(small_other, groups, 1)
    inner_parts = grad_call(
        inner_grad_kernel, [SMEM] + [VMEM] * 4, (part, hidden), "inner_grad",
    )(me, mine, given, after(hidden_low, grads), hidden_given)
    direct = groups == 8 and lax.axis_size("rep") == 4
    if direct:
        first_sum = group_sum(outer_parts, groups, inner_parts[0])
        first_copies = CopiesSum(first_sum)
        first_copies.start()
    waited = (first_copies.kept,) if direct else ()
    attention_parts = grad_call(
        attention_grad_kernel, [SMEM] + [VMEM] * 8,
        (4 * part + SMALL_ROWS, width), "attention_grad",
    )(me, after(mine, *waited), given, grads, grads_given, branch, branch_given, small_mine, small_given)
    if direct:
        first_pair = first_copies.cross(attention_parts[0])
        second_sum = group_sum(inner_parts, groups, first_pair)
        second_copies = CopiesSum(second_sum)
        second_copies.start()
        waited = (second_copies.kept,)
    (grad_tokens,) = call(
        functools.partial(grad_tokens_kernel, groups, shards),
        [SMEM, VMEM, VMEM] + [ANY] * len(shards.operands(0)),
        [((rows, width), BF16)],
        [pltpu.VMEM(weight, BF16)] * 3 + [pltpu.SemaphoreType.DMA((3 * groups,))],
        "grad_tokens",
    )(me, after(grads, *waited), grad_first, *shards.operands(0))

    if direct:
        first_total = first_copies.back(grad_tokens)
        second_pair = second_copies.cross(first_total)
        third_sum = group_sum(attention_parts, groups, second_pair)
        second_copies.back(third_sum)
        (grad_outer,) = first_copies.results((0, width))
        (grad_inner,) = second_copies.results((0, hidden))
        grad_attention = copies_sum(third_sum, grad_outer, grad_inner)
    else:
        grad_outer, grad_inner, grad_attention = [
            lax.psum(group_sum_any(piece[0], groups).astype(BF16), "rep").astype(F32)
            for piece in (outer_parts, inner_parts, attention_parts)]
    return (
        layer_out,
        grad_tokens,
        grad_attention[:part],
        grad_attention[part : 2 * part],
        grad_attention[2 * part : 3 * part],
        grad_attention[3 * part : 4 * part],
        grad_inner,
        grad_outer,
    ) + tuple(grad_attention[4 * part + row, : piece.shape[0]] for row, piece in enumerate(smalls))


def solution(mesh):
    split = P(("dp", "rep"), None)
    rows = P("dp", None)
    vector = P("dp")
    return jax.shard_map(
        local,
        mesh=mesh,
        in_specs=(split,) * 3 + (rows,) * 6 + (vector,) * 9,
        out_specs=(split,) * 2 + (rows,) * 6 + (vector,) * 9,
        check_vma=False,
    )
```

```python
import functools

import jax
import jax.numpy as jnp
from jax import lax
from jax.experimental import pallas as pl
from jax.experimental.pallas import tpu as pltpu
from jax.sharding import PartitionSpec as P

HEADS = 8
HEAD_DIM = 64
EPS = 1e-05
SMALL_ROWS = 16
BF16 = jnp.bfloat16
F32 = jnp.float32
VMEM_LIMIT = 56 * 1024 * 1024


def dot(left, right):
    return lax.dot_general(left, right, (((1,), (0,)), ((), ())), preferred_element_type=F32)


def dot_rt(left, right):
    return lax.dot_general(left, right, (((1,), (1,)), ((), ())), preferred_element_type=F32)


def dot_lt(left, right):
    return lax.dot_general(left, right, (((0,), (0,)), ((), ())), preferred_element_type=F32)


def mean_of(values):
    return jnp.mean(values, -1, keepdims=True)


def normalize(summed):
    centred = summed - mean_of(summed)
    scale = lax.rsqrt(mean_of(centred * centred) + EPS)
    return centred * scale, scale


def norm_back(grad_normed, normed, scale):
    return scale * (grad_normed - mean_of(grad_normed) - normed * mean_of(grad_normed * normed))


def row_sum(values):
    return jnp.sum(values, 0, keepdims=True)


class Shards:
    def __init__(self, arrays, places, stacked):
        self.arrays = arrays
        self.places = places
        self.stacked = stacked

    def used(self, kinds):
        if self.stacked:
            return [0]
        return sorted({index for kind in kinds for index, _ in self.places[kind]})

    def operands(self, *kinds):
        return [self.arrays[index] for index in self.used(kinds)]

    def sources(self, refs, groups, *kinds):
        used = self.used(kinds)
        if self.stacked:
            return [[(refs[0].at[index], self.places[kind]) for index in range(groups)]
                    for kind in kinds], refs[1:]
        found = dict(zip(used, refs))
        return [[(found[index], row) for index, row in self.places[kind]]
                for kind in kinds], refs[len(used) :]


def load(me, sources, relative, pieces, sems, base):
    copies = []
    for index, (source, start) in enumerate(sources):
        owner = (me ^ index) if relative else index
        for first, size, target, column in pieces:
            place = owner * size
            if relative:
                place = pl.multiple_of(place, size)
            where = target.at[pl.ds(place, size)]
            if column is not None:
                where = target.at[pl.ds(place, size), pl.ds(*column)]
            if isinstance(start, tuple):
                chosen = source.at[pl.ds(start[0], size), pl.ds(*column)]
            else:
                chosen = source.at[pl.ds(start + first, size)]
            copies.append(pltpu.make_async_copy(chosen, where, sems.at[base + len(copies)]))
    return copies


def inner_pieces(part, wi):
    width = wi.shape[0]
    return [(index * part, part, wi, (index * width, width))
            for index in range(wi.shape[1] // width)]


def ends_of(len_ref, slots):
    ends = []
    total = jnp.int32(0)
    for slot in range(slots):
        total = total + len_ref[0, slot]
        ends.append(total)
    return ends


def valid_rows(len_ref, rows):
    ends = ends_of(len_ref, len_ref.shape[1])
    places = lax.broadcasted_iota(jnp.int32, (rows, 1), 0)
    return (places < ends[-1]).astype(F32)


def pack_kernel(count, *refs):
    sources = refs[: 4 + count]
    first_ref = refs[4 + count]
    small_refs = refs[5 + count : -1]
    sems = refs[-1]
    part, width = sources[0].shape
    pairs = [(source, first_ref.at[pl.ds(index * part, part)])
             for index, source in enumerate(sources[:4])]
    pairs += list(zip(sources[4:], small_refs))
    copies = [
        pltpu.make_async_copy(source, target, sems.at[index])
        for index, (source, target) in enumerate(pairs)]
    for copy in copies:
        copy.start()
    for copy in copies:
        copy.wait()
    rows = []
    for small in small_refs:
        values = small[...].astype(F32)
        pieces = [values[row : row + 1] for row in range(values.shape[0])]
        filled = values.shape[0] * values.shape[1]
        rows.append(jnp.concatenate(pieces + [jnp.zeros((1, width - filled), F32)], 1))
    rows.append(jnp.zeros((SMALL_ROWS - len(rows), width), F32))
    first_ref[4 * part :] = jnp.concatenate(rows, 0).astype(BF16)


def forward_attention_kernel(
    groups, shards, me_ref, len_ref, tok_any, *refs
):
    relative = not shards.stacked
    (first_sources,), refs = shards.sources(refs, groups, 0)
    (query_ref, key_ref, value_ref, probs_ref, normed_ref, scale_ref, vec_ref, mine_ref, other_ref,
     wq, wk, wv, wo, smalls, joined, turned, tok_ref, sems) = refs
    me = me_ref[0]
    rows, width = tok_ref.shape
    part = width // groups
    copies = load(me, first_sources, relative, [
        (0, part, wq, None), (part, part, wk, None), (2 * part, part, wv, None),
        (3 * part, part, wo, None), (4 * part, SMALL_ROWS, smalls, None)], sems, 0)
    fetch = pltpu.make_async_copy(tok_any, tok_ref, sems.at[len(copies)])
    fetch.start()
    for kind in (4, 0, 1, 2, 3):
        for copy in copies[kind::5]:
            copy.start()
    fetch.wait()
    tokens = tok_ref[...]
    ends = ends_of(len_ref, len_ref.shape[1])
    across = lax.broadcasted_iota(jnp.int32, (rows, rows), 1)
    down = lax.broadcasted_iota(jnp.int32, (rows, rows), 0)
    segment_across = jnp.zeros((rows, rows), jnp.int32)
    segment_down = jnp.zeros((rows, rows), jnp.int32)
    for end in ends:
        segment_across = segment_across + (across >= end).astype(jnp.int32)
        segment_down = segment_down + (down >= end).astype(jnp.int32)
    same = segment_across == segment_down
    turned[0] = tokens.astype(F32).T.astype(BF16).reshape(groups // 2, 2, part, rows)
    for copy in copies[4::5] + copies[0::5]:
        copy.wait()
    ff_part = vec_ref.shape[1] // groups
    vec_ref[...] = jnp.zeros_like(vec_ref)
    for owner in range(groups):
        block = smalls[owner * SMALL_ROWS : (owner + 1) * SMALL_ROWS].astype(F32)
        for row in range(9):
            size = ff_part if row == 3 else part
            vec_ref[row : row + 1, owner * size : (owner + 1) * size] = block[row : row + 1, :size]
    query = (dot(tokens, wq[...]) + vec_ref[0:1, :width]).astype(BF16)
    for copy in copies[1::5]:
        copy.wait()
    keys = dot(tokens, wk[...]).astype(BF16)
    for copy in copies[2::5]:
        copy.wait()
    values = (dot(tokens, wv[...]) + vec_ref[1:2, :width]).astype(BF16)
    query_ref[...] = query
    key_ref[...] = keys
    value_ref[...] = values
    for head in range(HEADS):
        lanes = slice(head * HEAD_DIM, (head + 1) * HEAD_DIM)
        scores = dot_rt(keys[:, lanes], query[:, lanes]) * HEAD_DIM ** (-0.5)
        scores = jnp.where(same, scores, -1e30)
        raised = jnp.exp(scores - jnp.max(scores, 0, keepdims=True))
        probs = (raised * (1.0 / jnp.sum(raised, 0, keepdims=True))).astype(BF16)
        probs_ref[head] = probs
        joined[:, lanes] = dot_lt(probs, values[:, lanes]).astype(BF16)
    for copy in copies[3::5]:
        copy.wait()
    attended = joined[...]
    summed = tokens.astype(F32) + dot(attended, wo[...]) + vec_ref[2:3, :width]
    normed, scale = normalize(summed)
    normed_ref[...] = normed
    scale_ref[...] = scale
    first_low = normed * vec_ref[5:6, :width] + vec_ref[6:7, :width]
    turned[1] = attended.astype(F32).T.astype(BF16).reshape(groups // 2, 2, part, rows)
    turned[2] = first_low.astype(BF16).astype(F32).T.astype(BF16).reshape(groups // 2, 2, part, rows)
    core = me & 1
    for kind in range(3):
        for block in range(groups // 2):
            mine_ref[kind, block] = turned[kind, block, core]
            other_ref[kind, block] = turned[kind, block, 1 - core]


def hidden_kernel(
    groups, shards, me_ref, len_ref, normed_any, scale_any, vec_any, cot_any, *refs
):
    relative = not shards.stacked
    (first_sources, inner_sources, outer_sources), refs = shards.sources(refs, groups, 0, 1, 2)
    (out_ref, low_ref, mine_ref, other_ref, hidden_ref, branch_ref, first_ref, att_ref, sums_ref, hidden_sum_ref,
     wi, wo, wb, slopes, kept, normed_ref, scale_ref, vec_ref, cot_ref, sems) = refs
    me = me_ref[0]
    rows, width = normed_ref.shape
    hidden = vec_ref.shape[1]
    part = width // groups
    ff_part = hidden // groups
    copies = load(me, inner_sources, relative, inner_pieces(part, wi), sems, 0)
    more = load(me, outer_sources, relative, [(0, ff_part, wo, None)], sems, len(copies))
    last = load(
        me, first_sources, relative, [(3 * part, part, wb, None)], sems, len(copies) + len(more))
    count = len(copies) + len(more) + len(last)
    inputs = [
        pltpu.make_async_copy(source, target, sems.at[count + index])
        for index, (source, target) in enumerate((
            (normed_any, normed_ref), (vec_any, vec_ref), (scale_any, scale_ref),
            (cot_any, cot_ref)))]
    for copy in inputs:
        copy.start()
    for chunk in range(hidden // width):
        for copy in copies[chunk :: hidden // width]:
            copy.start()
    for copy in more + last:
        copy.start()
    for copy in inputs:
        copy.wait()
    first_normed = normed_ref[...]
    first_out = first_normed * vec_ref[5:6, :width] + vec_ref[6:7, :width]
    first_low = first_out.astype(BF16)
    core = me & 1
    for start in range(0, hidden, width):
        lanes = slice(start, start + width)
        for copy in copies[start // width :: hidden // width]:
            copy.wait()
        inner = dot(first_low, wi[:, lanes]) + vec_ref[3:4, lanes]
        below = 0.5 * (1.0 + lax.erf(inner * 0.7071067811865476))
        slopes[:, lanes] = below + inner * jnp.exp(-0.5 * inner * inner) * 0.3989422804014327
        activated = (inner * below).astype(BF16)
        for owner in range(start // ff_part, (start + width) // ff_part):
            first = owner * ff_part - start
            kept[owner // 2, owner % 2] = activated[:, first : first + ff_part]
    for copy in more:
        copy.wait()
    second_sum = first_out + vec_ref[4:5, :width]
    for owner in range(groups):
        second_sum = second_sum + dot(
            kept[owner // 2, owner % 2], wo[owner * ff_part : (owner + 1) * ff_part])
    normed, scale = normalize(second_sum)
    valid = valid_rows(len_ref, rows)
    gain = vec_ref[7:8, :width]
    out_ref[...] = (valid * (normed * gain + vec_ref[8:9, :width])).astype(BF16)
    upstream = cot_ref[...].astype(F32) * valid
    grad = norm_back(upstream * gain, normed, scale)
    low = grad.astype(BF16)
    low_ref[...] = low
    sums_ref[0:1] = row_sum(low.astype(F32))
    sums_ref[1:2] = row_sum(upstream * normed)
    sums_ref[2:3] = row_sum(upstream)
    for block in range(groups // 2):
        mine_ref[block] = kept[block, core]
        other_ref[block] = kept[block, 1 - core]
    for start in range(0, hidden, width):
        lanes = slice(start, start + width)
        inner_low = (dot_rt(low, wo[lanes]) * slopes[:, lanes]).astype(BF16)
        hidden_ref[:, lanes] = inner_low
        hidden_sum_ref[:, lanes] = row_sum(inner_low.astype(F32))
    grad_out = grad + dot_rt(hidden_ref[...], wi[...])
    sums_ref[3:4] = row_sum(grad_out * first_normed)
    sums_ref[4:5] = row_sum(grad_out)
    grad_first = norm_back(grad_out * vec_ref[5:6, :width], first_normed, scale_ref[...])
    branch = grad_first.astype(BF16)
    sums_ref[5:6] = row_sum(branch.astype(F32))
    first_ref[...] = grad_first
    branch_ref[...] = branch
    for copy in last:
        copy.wait()
    att_ref[...] = dot_rt(branch, wb[...]).astype(BF16)


def backward_attention_kernel(
    groups, me_ref, query_ref, key_ref, value_ref, probs_ref, att_ref,
    sums, hidden_sums, grads_ref, mine_ref, other_ref, packed
):
    rows, width = query_ref.shape
    hidden = hidden_sums.shape[1]
    part = width // groups
    ff_part = hidden // groups
    for head in range(HEADS):
        lanes = slice(head * HEAD_DIM, (head + 1) * HEAD_DIM)
        grad_att = att_ref[:, lanes]
        probs = probs_ref[head].astype(F32)
        grad_probs = dot_rt(value_ref[:, lanes], grad_att)
        mixed = probs * grad_probs
        grad_scores = (mixed - probs * jnp.sum(mixed, 0, keepdims=True)).astype(BF16)
        scale = HEAD_DIM ** (-0.5)
        for kind, grad in enumerate((
            scale * dot_lt(grad_scores, key_ref[:, lanes]),
            scale * dot(grad_scores, query_ref[:, lanes]),
            dot(probs_ref[head], grad_att),
        )):
            first = kind * width + head * HEAD_DIM
            grads_ref[:, first : first + HEAD_DIM] = grad.astype(BF16)
    packed[...] = jnp.zeros_like(packed)
    query_sum = row_sum(grads_ref[:, :width].astype(F32))
    value_sum = row_sum(grads_ref[:, 2 * width :].astype(F32))
    ordered = (
        query_sum, value_sum, sums[5:6], hidden_sums[0:1], sums[0:1],
        sums[3:4], sums[4:5], sums[1:2], sums[2:3])
    for owner in range(groups):
        for row, vector in enumerate(ordered):
            size = ff_part if row == 3 else part
            packed[owner // 2, owner % 2, row : row + 1, :size] = vector[
                :, owner * size : (owner + 1) * size]
    core = me_ref[0] & 1
    for block in range(groups // 2):
        mine_ref[block] = packed[block, core]
        other_ref[block] = packed[block, 1 - core].astype(BF16)


def grad_tokens_kernel(groups, shards, me_ref, grads_ref, first_ref, *refs):
    relative = not shards.stacked
    (first_sources,), refs = shards.sources(refs, groups, 0)
    out_ref, wq, wk, wv, sems = refs
    me = me_ref[0]
    rows, width = first_ref.shape
    part = width // groups
    copies = load(me, first_sources, relative, [
        (0, part, wq, None), (part, part, wk, None), (2 * part, part, wv, None)], sems, 0)
    for copy in copies:
        copy.start()
    for copy in copies:
        copy.wait()
    total = first_ref[...]
    for kind, weight in enumerate((wq, wk, wv)):
        total = total + dot_rt(grads_ref[:, kind * width : (kind + 1) * width], weight[...])
    out_ref[...] = total.astype(BF16)


def put(refs, blocks, slot, start, lanes, value):
    ref = refs[slot] if blocks == 4 else refs[0].at[slot]
    ref[start : start + value.shape[0], lanes] = value.astype(ref.dtype)


def outer_grad_kernel(blocks, me_ref, mine_ref, given_ref, low_ref, low_given_ref, *refs):
    first = me_ref[0] >> 1 if blocks == 4 else 0
    low = jnp.concatenate([low_ref[...], low_given_ref[...]], 0)
    for slot in range(blocks):
        block = slot ^ first
        acts = jnp.concatenate([mine_ref[block], given_ref[block]], 0)
        put(refs, blocks, slot, 0, slice(None), dot_lt(acts, low))


def inner_grad_kernel(blocks, me_ref, mine_ref, given_ref, low_ref, low_given_ref, *refs):
    first = me_ref[0] >> 1 if blocks == 4 else 0
    left = jnp.concatenate([
        jnp.concatenate([mine_ref[2, slot ^ first], given_ref[2, slot ^ first]], 1)
        for slot in range(blocks)], 0)
    part = left.shape[0] // blocks
    step = 512
    for start in range(0, low_ref.shape[1], step):
        lanes = slice(start, start + step)
        low = jnp.concatenate([low_ref[:, lanes], low_given_ref[:, lanes]], 0)
        grad = dot(left, low)
        for slot in range(blocks):
            put(refs, blocks, slot, 0, lanes, grad[slot * part : (slot + 1) * part])


def attention_grad_kernel(
    blocks, me_ref, mine_ref, given_ref, grads_ref, grads_given_ref, branch_ref, branch_given_ref,
    small_ref, small_given_ref, *refs
):
    first = me_ref[0] >> 1 if blocks == 4 else 0
    width = branch_ref.shape[1]
    lefts = [
        jnp.concatenate([
            jnp.concatenate([mine_ref[kind, slot ^ first], given_ref[kind, slot ^ first]], 1)
            for slot in range(blocks)], 0)
        for kind in range(2)]
    part = lefts[0].shape[0] // blocks
    for kind in range(4):
        if kind < 3:
            lanes = slice(kind * width, (kind + 1) * width)
            right = jnp.concatenate([grads_ref[:, lanes], grads_given_ref[:, lanes]], 0)
            grad = dot(lefts[0], right)
        else:
            grad = dot(lefts[1], jnp.concatenate([branch_ref[...], branch_given_ref[...]], 0))
        for slot in range(blocks):
            put(refs, blocks, slot, kind * part, slice(None), grad[slot * part : (slot + 1) * part])
    for slot in range(blocks):
        small = small_ref[slot ^ first] + small_given_ref[slot ^ first].astype(F32)
        put(refs, blocks, slot, 4 * part, slice(None), small)


ANY = pl.BlockSpec(memory_space=pl.ANY)
HBM = pl.BlockSpec(memory_space=pltpu.HBM)
VMEM = pl.BlockSpec(memory_space=pltpu.VMEM)
SMEM = pl.BlockSpec(memory_space=pltpu.SMEM)


def call(kernel, in_specs, outs, scratch, name):
    return pl.pallas_call(
        kernel,
        out_shape=[jax.ShapeDtypeStruct(shape, dtype) for shape, dtype in outs],
        in_specs=in_specs,
        out_specs=[VMEM] * len(outs),
        scratch_shapes=scratch,
        compiler_params=pltpu.CompilerParams(vmem_limit_bytes=VMEM_LIMIT),
        cost_estimate=pl.CostEstimate(flops=2_000_000_000, bytes_accessed=8_000_000, transcendentals=0),
        name=name,
    )


def after(value, *others):
    return lax.optimization_barrier((value,) + others)[0]


def flip(groups, mask):
    return [(index, index ^ mask) for index in range(groups)]


def swap(value, groups, mask):
    return lax.ppermute(value, "dp", flip(groups, mask))


def swapped(value, groups):
    return [value, swap(value, groups, 1)]


def group_sum(parts, groups, *others):
    keep = parts[0]
    got = [swap(sent, groups, mask) for mask, sent in zip((2, 4, 6), parts[1:])]
    got = lax.optimization_barrier(tuple(got) + others)[:3]
    return keep.astype(F32) + got[0].astype(F32) + got[1].astype(F32) + got[2].astype(F32)


def group_sum_any(stacked, groups):
    core = lax.axis_index("dp") & 1
    blocks = groups // 2
    full = jnp.zeros((blocks, 2) + stacked.shape[1:], stacked.dtype)
    full = lax.dynamic_update_slice_in_dim(full, stacked[:, None], core, 1)
    full = full.reshape((groups,) + stacked.shape[1:])
    return lax.psum_scatter(full, "dp", scatter_dimension=0, tiled=False).astype(F32)


class CopiesSum:
    near = [(0, 1), (1, 0), (2, 3), (3, 2)]
    far = [(0, 2), (2, 0), (1, 3), (3, 1)]

    def __init__(self, value):
        self.value = value.astype(BF16)
        self.upper = lax.axis_index("rep") & 1
        self.half = value.shape[0] // 2

    def start(self, *others):
        value = after(self.value, *others)
        self.kept = lax.dynamic_slice_in_dim(value, self.upper * self.half, self.half)
        sent = lax.dynamic_slice_in_dim(value, (1 - self.upper) * self.half, self.half)
        self.got = lax.ppermute(sent, "rep", self.near)

    def cross(self, *others):
        got = after(self.got, *others)
        self.pair = (self.kept.astype(F32) + got.astype(F32)).astype(BF16)
        self.got = lax.ppermute(self.pair, "rep", self.far)
        return self.pair

    def back(self, *others):
        got = after(self.got, *others)
        self.total = (self.pair.astype(F32) + got.astype(F32)).astype(BF16)
        self.got = lax.ppermute(self.total, "rep", self.near)
        return self.total

    def results(self, *columns):
        lower = self.upper == 0
        found = []
        for start, end in columns:
            total, got = self.total[:, start:end], self.got[:, start:end]
            halves = [jnp.where(lower, total, got), jnp.where(lower, got, total)]
            found.append(jnp.concatenate(halves).astype(F32))
        return found


def local(
    tokens,
    cotangent,
    seq_lengths,
    query_weight,
    key_weight,
    value_weight,
    output_weight,
    inner_weight,
    outer_weight,
    query_bias,
    value_bias,
    output_bias,
    inner_bias,
    outer_bias,
    first_gain,
    first_shift,
    second_gain,
    second_shift,
):
    groups = lax.axis_size("dp")
    blocks = groups // 2
    rows, width = tokens.shape
    part = width // groups
    ff_part = outer_weight.shape[0]
    hidden = ff_part * groups
    me = lax.axis_index("dp").astype(jnp.int32).reshape(1)
    smalls = (
        query_bias,
        value_bias,
        output_bias,
        inner_bias,
        outer_bias,
        first_gain,
        first_shift,
        second_gain,
        second_shift,
    )
    small_inputs = [
        piece.reshape(max(1, piece.shape[0] // 128), min(128, piece.shape[0])) for piece in smalls]
    first_rows = 4 * part + SMALL_ROWS
    (first_own,) = call(
        functools.partial(pack_kernel, len(smalls)),
        [HBM] * (4 + len(smalls)),
        [((first_rows, width), BF16)],
        [pltpu.VMEM(piece.shape, BF16) for piece in small_inputs]
        + [pltpu.SemaphoreType.DMA((4 + len(smalls),))],
        "pack",
    )(query_weight, key_weight, value_weight, output_weight, *small_inputs)
    if groups == 8:
        inner_y = swap(inner_weight, groups, 4)
        outer_x = swap(outer_weight, groups, 2)
        first_hops = [swap(first_own, groups, mask) for mask in (6, 2, 4)]
        own = (first_own, inner_weight, outer_weight)
        *hops, first_pair, inner_pair, outer_pair = lax.optimization_barrier(
            (*first_hops, inner_y, outer_x) + tuple(swap(value, groups, 1) for value in own))
        inner_x = swap(jnp.concatenate([inner_weight, hops[3]]), groups, 2)
        outer_y = swap(jnp.concatenate([outer_weight, hops[4]]), groups, 4)
        arrays = [first_own, first_pair, inner_weight, inner_pair, outer_weight, outer_pair]
        for value in hops:
            arrays.extend(swapped(value, groups))

        def spread(*found):
            return [(2 * index + core, row) for index, row in found for core in range(2)]

        shards = Shards(arrays, (
            spread((0, 0), (4, 0), (5, 0), (3, 0)),
            spread((1, (0,)), (8, (0,)), (6, (0,)), (8, (part,))),
            spread((2, 0), (7, 0), (9, 0), (9, ff_part))), False)
    else:
        blocked = inner_weight.reshape(part, hidden // width, width).swapaxes(0, 1)
        packed = jnp.concatenate([first_own, blocked.reshape(-1, width), outer_weight])
        shards = Shards([lax.all_gather(packed, "dp", axis=0, tiled=False)],
                        (0, first_rows, packed.shape[0] - ff_part), True)
    weight = (width, width)
    turned = (3, blocks, part, rows)
    query, keys, values, probs, normed, scale, vectors, mine, other = call(
        functools.partial(forward_attention_kernel, groups, shards),
        [SMEM, SMEM] + [ANY] * (1 + len(shards.operands(0))),
        [((rows, width), BF16)] * 3
        + [((HEADS, rows, rows), BF16), ((rows, width), F32), ((rows, 1), F32),
           ((SMALL_ROWS, hidden), F32), (turned, BF16), (turned, BF16)],
        [pltpu.VMEM(weight, BF16)] * 4
        + [pltpu.VMEM((groups * SMALL_ROWS, width), BF16), pltpu.VMEM((rows, width), BF16),
           pltpu.VMEM((3, blocks, 2, part, rows), BF16), pltpu.VMEM((rows, width), BF16),
           pltpu.SemaphoreType.DMA((5 * groups + 1,))],
        "forward_attention",
    )(me, seq_lengths, tokens, *shards.operands(0))
    given = swap(other, groups, 1)
    if groups == 8:
        inner_x, outer_y, arrays[13], arrays[15] = lax.optimization_barrier(
            (inner_x, outer_y, arrays[13], arrays[15], normed))[:4]
        for value in (inner_x, outer_y):
            arrays.extend(swapped(value, groups))
    acts = (blocks, rows, ff_part)
    (layer_out, outer_low, act_mine, act_other, hidden_low, branch, grad_first, grad_att, sums,
     hidden_sums) = call(
        functools.partial(hidden_kernel, groups, shards),
        [SMEM, SMEM] + [ANY] * (4 + len(shards.operands(0, 1, 2))),
        [((rows, width), BF16), ((rows, width), BF16), (acts, BF16), (acts, BF16),
         ((rows, hidden), BF16), ((rows, width), BF16), ((rows, width), F32), ((rows, width), BF16),
         ((8, width), F32), ((1, hidden), F32)],
        [pltpu.VMEM((width, hidden), BF16), pltpu.VMEM((hidden, width), BF16),
         pltpu.VMEM(weight, BF16), pltpu.VMEM((rows, hidden), F32),
         pltpu.VMEM((blocks, 2, rows, ff_part), BF16),
         pltpu.VMEM((rows, width), F32), pltpu.VMEM((rows, 1), F32),
         pltpu.VMEM((SMALL_ROWS, hidden), F32), pltpu.VMEM((rows, width), BF16),
         pltpu.SemaphoreType.DMA(((2 + hidden // width) * groups + 4,))],
        "hidden",
    )(me, seq_lengths, normed, scale, vectors, cotangent, *shards.operands(0, 1, 2))
    act_given = swap(act_other, groups, 1)
    outer_given = swap(outer_low, groups, 1)

    def grad_call(kernel, specs, shape, name):
        if blocks == 4:
            outs = [(shape, BF16)] * 4
        else:
            outs = [((blocks,) + shape, BF16)]
        return call(functools.partial(kernel, blocks), specs, outs, [], name)

    outer_parts = grad_call(
        outer_grad_kernel, [SMEM] + [VMEM] * 4, (ff_part, width), "outer_grad",
    )(me, act_mine, act_given, outer_low, outer_given)
    hidden_given = swap(after(hidden_low, outer_parts[0]), groups, 1)
    branch_given = swap(after(branch, outer_parts[0]), groups, 1)
    small = (blocks, SMALL_ROWS, width)
    grads, small_mine, small_other = call(
        functools.partial(backward_attention_kernel, groups),
        [SMEM] + [VMEM] * 7,
        [((rows, 3 * width), BF16), (small, F32), (small, BF16)],
        [pltpu.VMEM((blocks, 2, SMALL_ROWS, width), F32)],
        "backward_attention",
    )(me, query, keys, values, probs, after(grad_att, outer_parts[0]), sums, hidden_sums)
    grads_given = swap(grads, groups, 1)
    small_given = swap(small_other, groups, 1)
    inner_parts = grad_call(
        inner_grad_kernel, [SMEM] + [VMEM] * 4, (part, hidden), "inner_grad",
    )(me, mine, given, after(hidden_low, grads), hidden_given)
    direct = groups == 8 and lax.axis_size("rep") == 4
    if direct:
        first_sum = group_sum(outer_parts, groups, inner_parts[0])
        first_copies = CopiesSum(first_sum)
        first_copies.start()
    waited = (first_copies.kept,) if direct else ()
    attention_parts = grad_call(
        attention_grad_kernel, [SMEM] + [VMEM] * 8,
        (4 * part + SMALL_ROWS, width), "attention_grad",
    )(me, after(mine, *waited), given, grads, grads_given, branch, branch_given, small_mine, small_given)
    if direct:
        first_pair = first_copies.cross(attention_parts[0])
        second_sum = group_sum(inner_parts, groups, first_pair)
        second_copies = CopiesSum(second_sum)
        second_copies.start()
        waited = (second_copies.kept,)
    (grad_tokens,) = call(
        functools.partial(grad_tokens_kernel, groups, shards),
        [SMEM, VMEM, VMEM] + [ANY] * len(shards.operands(0)),
        [((rows, width), BF16)],
        [pltpu.VMEM(weight, BF16)] * 3 + [pltpu.SemaphoreType.DMA((3 * groups,))],
        "grad_tokens",
    )(me, after(grads, *waited), grad_first, *shards.operands(0))

    if direct:
        first_total = first_copies.back(grad_tokens)
        second_pair = second_copies.cross(first_total)
        third_sum = group_sum(attention_parts, groups, second_pair)
        third_copies = CopiesSum(third_sum)
        third_copies.start()
        second_total = second_copies.back(third_copies.kept)
        third_copies.cross(second_total)
        (grad_outer,) = first_copies.results((0, width))
        third_copies.back(grad_outer)
        (grad_inner,) = second_copies.results((0, hidden))
        third_copies.got = after(third_copies.got, grad_inner)
        (grad_attention,) = third_copies.results((0, width))
    else:
        grad_outer, grad_inner, grad_attention = [
            lax.psum(group_sum_any(piece[0], groups).astype(BF16), "rep").astype(F32)
            for piece in (outer_parts, inner_parts, attention_parts)]
    return (
        layer_out,
        grad_tokens,
        grad_attention[:part],
        grad_attention[part : 2 * part],
        grad_attention[2 * part : 3 * part],
        grad_attention[3 * part : 4 * part],
        grad_inner,
        grad_outer,
    ) + tuple(grad_attention[4 * part + row, : piece.shape[0]] for row, piece in enumerate(smalls))


def solution(mesh):
    split = P(("dp", "rep"), None)
    rows = P("dp", None)
    vector = P("dp")
    return jax.shard_map(
        local,
        mesh=mesh,
        in_specs=(split,) * 3 + (rows,) * 6 + (vector,) * 9,
        out_specs=(split,) * 2 + (rows,) * 6 + (vector,) * 9,
        check_vma=False,
    )
```
